128 devices in a mesh: ctx: 8 (over x, core), exp: 16 (over z, y).
Axes of the slice: x: 4, y: 4, z: 4, core: 2. Of those that a mesh axis runs over, the one named last changes fastest.
Arguments:
- hidden_in: bfloat16 [16384, 3584], P(('ctx', 'exp')), may hold values from -6 to 6
- queries: bfloat16 [16384, 3584], P(('ctx', 'exp')), may hold values from -21 to 21
- key_rows: bfloat16 [16384, 512], P(('ctx', 'exp')), may hold values from -6 to 6
- value_rows: bfloat16 [16384, 512], P(('ctx', 'exp')), may hold values from -6 to 6
- document_ids: int32 [16384], P(('ctx', 'exp')), may hold values from 0 to 127, never falling along the last dimension, each value on 1 to 384 neighbouring positions
- norm_gain: float32 [3584], replicated, may hold values from 0.1 to 1.9
- w_gate: bfloat16 [128, 3584, 640], P(('ctx', 'exp')), may hold values from -0.09375 to 0.09375
- w_up: bfloat16 [128, 3584, 640], P(('ctx', 'exp')), may hold values from -0.09375 to 0.09375
- w_down: bfloat16 [128, 640, 3584], P(('ctx', 'exp')), may hold values from -0.15625 to 0.15625
- expert_ids: int32 [16384, 8], P(('ctx', 'exp')), may hold values from 0 to 63, all different within a row; in each aligned block of 128 rows (0 to 127, 128 to 255, ...) at most 17 rows name the same one
- route_weights: float32 [16384, 8], P(('ctx', 'exp')), may hold values from 0.05 to 0.6
Outputs:
- layer_out: bfloat16 [16384, 3584], P(('ctx', 'exp'))
The draws below stay inside these ranges and needn't reach their ends.
Inputs may be any that keep to these rules, and one draw needn't show every extreme that they name: `document_ids`: document ids never fall along the row; each document has 1 to 384 positions and one has exactly 384. `expert_ids`: the 8 ids of a token are distinct. Among the 128 tokens of one device (aligned blocks of the row) no expert is named more than 17 times, and in every draw some expert is named exactly 17 times in some block.
All inputs are finite; a program needn't handle non-finite values.
Results may differ from the reference program's by a relative error of at most 0.015.
Values may be sent and summed in bfloat16 or wider, within the bound.
A program may use at most 192 MiB of HBM per device.

```python
import math
import jax
import jax.numpy as jnp
import numpy as np
from jax import lax

D = 3584
HEADS = 28
KV_HEADS = 4
HEAD_DIM = 128
TOPK = 8
FF = 1280
TOK_DEV = 128
WINDOW = 4
GROUP = 7
FF_HALF = 640
TOKENS = 16384
EXPERTS = 64
CAP = 17
DOC_MOST = 384
DOCS = 128
DEVICES = 128


def draw_queries(key, part):
    key = jax.random.fold_in(key, 11)
    result = jnp.clip(jax.random.normal(key, (TOKENS, HEADS * HEAD_DIM), jnp.float32), -6.0, 6.0)
    return result.astype(jnp.bfloat16)


def draw_key_rows(key, part):
    key = jax.random.fold_in(key, 13)
    result = jnp.clip(jax.random.normal(key, (TOKENS, KV_HEADS * HEAD_DIM), jnp.float32), -6.0, 6.0)
    return result.astype(jnp.bfloat16)


def levels(key, shape, split, smallest, high):
    factor_of, own = 1.0, jax.random.fold_in(key, 6)
    for dim, parts in split:
        steps = jnp.exp(jax.random.uniform(jax.random.fold_in(own, dim), (parts,), jnp.float32, smallest / len(split), high / len(split)))
        factor_of = factor_of * jnp.repeat(steps, shape[dim] // parts).reshape([-1 if axis == dim else 1 for axis in range(len(shape))])
    return factor_of


def length_profile(count, total, most, slope):
    loads = [(1 << 20) // math.isqrt(grade ** slope) + 1 for grade in range(2, count + 1)]
    spare, counts = total - most - (count - 1), [1] * (count - 1)
    while spare > 0:
        movable = [i for i in range(count - 1) if counts[i] < most]
        pool, remaining = sum([loads[i] for i in movable]), spare
        for i in movable:
            addition = min(most - counts[i], max(1, remaining * loads[i] // pool), spare)
            counts[i] = counts[i] + addition
            spare = spare - addition
    return np.array([most] + counts)


def ragged_sizes(own_key, number_of, total, bound, slope):
    if number_of == 2:
        one = jax.random.randint(own_key, (), max(1, total - bound), min(bound, total - 1) + 1)
        return jnp.stack([one, total - one])
    tallies = jnp.asarray(length_profile(number_of, total, bound, slope), jnp.int32)
    couples = (number_of - 1) // 2
    giver, taker = tallies[1:1 + 2 * couples:2], tallies[2:2 + 2 * couples:2]
    slack = jnp.minimum(giver - 1, bound - taker)
    passed = jax.random.randint(jax.random.fold_in(own_key, 1), (couples,), 0, 1 << 20) % (slack + 1)
    tallies = tallies.at[1:1 + 2 * couples:2].set(giver - passed).at[2:2 + 2 * couples:2].set(taker + passed)
    return tallies[jax.random.permutation(jax.random.fold_in(own_key, 2), number_of)]


def routed_block(rng, own, number, rows, count, top, reach, slope):
    ranking = jax.random.permutation(rng, count)
    heavy_load, usual = portions_of(count, rows * top, reach, slope, True), portions_of(count, rows * top, reach, slope, False)
    places = jnp.arange(count)

    def named(lengths, offset_by):
        used = int((lengths > 0).sum())
        fixed = max(1, used // 4)
        shifted = fixed + (places - fixed + offset_by * (used - fixed)) % max(1, count - fixed)
        return jnp.zeros((count,), jnp.int32).at[ranking[jnp.where(places < fixed, places, shifted)]].set(jnp.asarray(lengths, jnp.int32))

    lengths = jnp.where(number % 4 == 0, named(heavy_load, number // 4), named(usual, number - number // 4 - 1))
    mixed = jax.random.permutation(jax.random.fold_in(own, 3), count)
    donor, receiver = mixed[0:count // 2 * 2:2], mixed[1:count // 2 * 2:2]
    room = jnp.minimum(lengths[donor] - 1, reach - lengths[receiver]) // 2
    room = jnp.where((donor == ranking[0]) | (receiver == ranking[0]) | (lengths[receiver] == 0), 0, jnp.maximum(room, 0))
    shifted = jax.random.randint(jax.random.fold_in(own, 4), (count // 2,), 0, 1 << 20) % (room + 1)
    lengths = lengths.at[donor].add(-shifted).at[receiver].add(shifted)
    labels = jnp.searchsorted(jnp.cumsum(lengths), jnp.arange(rows * top), side="right").astype(jnp.int32)
    table = labels.reshape(top, rows).T
    table = table[jax.random.permutation(jax.random.fold_in(own, 1), rows)]
    offset_by = jax.random.randint(jax.random.fold_in(own, 2), (rows, 1), 0, top)
    return jnp.take_along_axis(table, (jnp.arange(top)[None, :] + offset_by) % top, axis=1)


def portions_of(count, total, bound, skew, full):
    weights = [(1 << 20) // math.isqrt(standing ** skew) + 1 for standing in range(1, count + 1)]
    largest = bound if full else min(bound, max(-(-total // count), total * weights[0] // sum(weights)))
    least = 1 if total - largest >= count - 1 else 0
    given, rest = [largest] + [least] * (count - 1), total - largest - least * (count - 1)
    while rest > 0:
        free = [i for i in range(1, count) if given[i] < largest] or [i for i in range(1, count) if given[i] < bound]
        mass, remaining = sum([weights[i] for i in free]), rest
        for i in free:
            extra = min(bound - given[i], max(1, remaining * weights[i] // mass), rest)
            given[i] = given[i] + extra
            rest = rest - extra
    return np.array(given)


def bell_draw(key, extent, spread, most, shards=(), kind=jnp.bfloat16):
    array = spread * jax.random.normal(key, extent, jnp.float32)
    if shards:
        array = array * levels(key, extent, shards, -0.22, 0.18)
    return jnp.clip(array, -most, most).astype(kind)


def setup_inputs(seed: int = 0) -> dict:
    key_of = jax.random.split(jax.random.key(seed), 12)
    hidden_in = bell_draw(key_of[0], (TOKENS, D), 1.0, 6.0, ((0, 128),))
    queries = draw_queries(jax.random.fold_in(key_of[11], 71), 0)
    key_rows = draw_key_rows(jax.random.fold_in(key_of[11], 71), 0)
    value_rows = bell_draw(key_of[3], (TOKENS, KV_HEADS * HEAD_DIM), 1.0, 6.0, ((0, 128),))
    document_ids = jnp.searchsorted(jnp.cumsum(ragged_sizes(key_of[4], DOCS, TOKENS, DOC_MOST, 2)), jnp.arange(TOKENS), side="right").astype(jnp.int32)
    norm_gain = jnp.clip(1.0 + 0.18 * jax.random.normal(key_of[5], (D,), jnp.float32), 0.1, 1.9)
    w_gate = bell_draw(key_of[6], (DEVICES, D, FF_HALF), D ** -0.5, 0.09375, ((0, 128),))
    w_up = bell_draw(key_of[7], (DEVICES, D, FF_HALF), D ** -0.5, 0.09375, ((0, 128),))
    w_down = bell_draw(key_of[8], (DEVICES, FF_HALF, D), FF ** -0.5, 0.15625, ((0, 128),))
    expert_ids_keys = jax.random.split(jax.random.fold_in(key_of[9], 1), TOKENS // TOK_DEV)
    expert_ids_turns = jax.random.permutation(jax.random.fold_in(key_of[9], 3), TOKENS // TOK_DEV)
    expert_ids = jax.vmap(lambda own, number: routed_block(jax.random.fold_in(key_of[9], 2), own, number, TOK_DEV, EXPERTS, TOPK, CAP, 2))(expert_ids_keys, expert_ids_turns).reshape((TOKENS, TOPK))
    route_weights = jnp.clip(jnp.exp(math.log(0.6) - 2.4849067 * jax.random.uniform(key_of[10], (TOKENS, TOPK), jnp.float32) ** levels(key_of[10], (TOKENS, TOPK), ((0, 128),), -0.2, 0.2)), 0.05, 0.6)
    return {"hidden_in": hidden_in, "queries": queries, "key_rows": key_rows, "value_rows": value_rows, "document_ids": document_ids, "norm_gain": norm_gain, "w_gate": w_gate, "w_up": w_up, "w_down": w_down, "expert_ids": expert_ids, "route_weights": route_weights}


masked_score = -1e+30

def attend_block(query_block, key_window, value_window, query_docs, key_docs, query_pos, key_pos):
    count = query_block.shape[0]
    query_heads = query_block.astype(jnp.float32).reshape(count, KV_HEADS, GROUP, HEAD_DIM)
    key_heads = key_window.astype(jnp.float32).reshape(-1, KV_HEADS, HEAD_DIM)
    value_heads = value_window.astype(jnp.float32).reshape(-1, KV_HEADS, HEAD_DIM)
    scores = jnp.einsum('qkgd,pkd->kgqp', query_heads, key_heads) * HEAD_DIM ** (-0.5)
    visible = (query_docs[:, None] == key_docs[None, :]) & (key_pos[None, :] <= query_pos[:, None])
    scores = jnp.where(visible[None, None], scores, masked_score)
    top = lax.optimization_barrier(jnp.max(scores, 3, keepdims=True))
    exps = jnp.exp(scores - top)
    probs = (exps / lax.optimization_barrier(jnp.sum(exps, 3, keepdims=True))).astype(jnp.bfloat16)
    context = jnp.einsum('kgqp,pkd->qkgd', probs.astype(jnp.float32), value_heads)
    return context.reshape(count, D).astype(jnp.bfloat16)

def reference(hidden_in, queries, key_rows, value_rows, document_ids, norm_gain, w_gate, w_up, w_down, expert_ids, route_weights):
    lead = (WINDOW - 1) * TOK_DEV
    key_pad = jnp.concatenate([jnp.zeros((lead, KV_HEADS * HEAD_DIM), key_rows.dtype), key_rows], 0)
    value_pad = jnp.concatenate([jnp.zeros((lead, KV_HEADS * HEAD_DIM), value_rows.dtype), value_rows], 0)
    doc_pad = jnp.concatenate([jnp.full((lead,), -1, jnp.int32), document_ids.astype(jnp.int32)], 0)

    def one_block(block_index):
        start = (block_index * TOK_DEV).astype(jnp.int32)
        query_block = lax.dynamic_slice_in_dim(queries, start, TOK_DEV, 0)
        key_window = lax.dynamic_slice_in_dim(key_pad, start, WINDOW * TOK_DEV, 0)
        value_window = lax.dynamic_slice_in_dim(value_pad, start, WINDOW * TOK_DEV, 0)
        query_docs = lax.dynamic_slice_in_dim(document_ids.astype(jnp.int32), start, TOK_DEV, 0)
        key_docs = lax.dynamic_slice_in_dim(doc_pad, start, WINDOW * TOK_DEV, 0)
        query_pos = start + jnp.arange(TOK_DEV, dtype=jnp.int32)
        key_pos = start - lead + jnp.arange(WINDOW * TOK_DEV, dtype=jnp.int32)
        return attend_block(query_block, key_window, value_window, query_docs, key_docs, query_pos, key_pos)
    context = lax.map(one_block, jnp.arange(DEVICES, dtype=jnp.int32)).reshape(TOKENS, D)
    resid = (hidden_in.astype(jnp.float32) + context.astype(jnp.float32)).astype(jnp.bfloat16)
    resid_f = resid.astype(jnp.float32)
    inverse = lax.rsqrt(lax.optimization_barrier(jnp.mean(resid_f * resid_f, 1, keepdims=True)) + 1e-06)
    normed = (resid_f * inverse * norm_gain[None, :]).astype(jnp.bfloat16)
    normed_pad = jnp.concatenate([normed, jnp.zeros((1, D), jnp.bfloat16)], 0)
    flat_ids = expert_ids.astype(jnp.int32).reshape(DEVICES, TOK_DEV * TOPK)
    onehot = (flat_ids[:, :, None] == jnp.arange(EXPERTS, dtype=jnp.int32)[None, None, :]).astype(jnp.int32)
    before = jnp.cumsum(onehot, 1) - onehot
    slot_in = lax.optimization_barrier(jnp.sum(before * onehot, 2))
    source = jnp.arange(DEVICES, dtype=jnp.int32)[:, None]
    position = (source * CAP + slot_in).reshape(-1).astype(jnp.int32)
    flat_all = flat_ids.reshape(-1)
    token_of = (jnp.arange(TOKENS * TOPK, dtype=jnp.int32) // TOPK).astype(jnp.int32)
    weight_flat = route_weights.reshape(-1)
    buffer_len = DEVICES * CAP

    def one_expert(total, expert):
        hit = flat_all == expert
        where_to = jnp.where(hit, position, buffer_len).astype(jnp.int32)
        slot_token = jnp.full((buffer_len,), TOKENS, jnp.int32).at[where_to].set(token_of, mode='drop')
        slot_weight = jnp.zeros((buffer_len,), jnp.float32).at[where_to].set(weight_flat, mode='drop')
        rows_in = normed_pad[slot_token]
        output = jnp.zeros((buffer_len, D), jnp.float32)
        for half in range(2):
            index = (2 * expert + half).astype(jnp.int32)
            gate_w = lax.dynamic_index_in_dim(w_gate, index, 0, keepdims=False)
            up_w = lax.dynamic_index_in_dim(w_up, index, 0, keepdims=False)
            down_w = lax.dynamic_index_in_dim(w_down, index, 0, keepdims=False)
            gate_act = jnp.dot(rows_in, gate_w, preferred_element_type=jnp.float32)
            up_act = jnp.dot(rows_in, up_w, preferred_element_type=jnp.float32)
            inner = (jax.nn.silu(gate_act) * up_act).astype(jnp.bfloat16)
            part = jnp.dot(inner, down_w, preferred_element_type=jnp.float32).astype(jnp.bfloat16)
            part = lax.optimization_barrier(part)
            output = output + part.astype(jnp.float32)
        total = total.at[slot_token].add(slot_weight[:, None] * output, mode='drop')
        return (total, None)
    moe, _ = lax.scan(one_expert, jnp.zeros((TOKENS, D), jnp.float32), jnp.arange(EXPERTS, dtype=jnp.int32))
    return (resid_f + moe).astype(jnp.bfloat16)
```

```python
import jax
import jax.numpy as jnp
from jax import lax
from jax.experimental import pallas as pl
from jax.experimental.pallas import tpu as pltpu
from jax.sharding import PartitionSpec as P

D = 3584
KV_HEADS = 4
HEAD_DIM = 128
TOPK = 8
WINDOW = 4
GROUP = 7
TOK = 128
CAP = 17
FF_HALF = 640
NQ = 7
CW = D // NQ
HW = CW // 2
SLAB = 144
NB = 2

MESH = pl.DeviceIdType.MESH
masked_score = -1e30
bf16 = jnp.bfloat16
f32 = jnp.float32


def coords():
    ctx, ex = lax.axis_index("ctx"), lax.axis_index("exp")
    return ctx // 2, ctx % 2, ex // 4, ex % 4


def place(x, c, z, y):
    return (x * 2 + c, z * 4 + y)


def greet(partners):
    barrier = pltpu.get_barrier_semaphore()
    for partner in partners:
        pl.semaphore_signal(barrier, inc=1, device_id=partner, device_id_type=MESH)
    pl.semaphore_wait(barrier, len(partners))


def remote(src, dst, send_sem, recv_sem, device):
    return pltpu.make_async_remote_copy(
        src_ref=src,
        dst_ref=dst,
        send_sem=send_sem,
        recv_sem=recv_sem,
        device_id=device,
        device_id_type=MESH,
    )


def plus(value, steps):
    return lax.rem(value + steps, 4)


def attend_kernel(
    hid, q, k, v, doc_row, doc_col, meta, gain,
    resid_out, nrm_out, meta_out,
    kw, vw, docw, halo_ss, halo_rs, meta_ss, meta_rs,
):
    x, c, z, y = coords()
    rank = lax.axis_index("ctx") * 16 + lax.axis_index("exp")

    def by_rank(steps):
        other = lax.rem(rank + steps + 128, 128)
        return (other // 16, lax.rem(other, 16))

    group = [(dc, dy) for dc in range(2) for dy in range(4) if (dc, dy) != (0, 0)]
    peers = [place(x, lax.rem(c + dc, 2), z, plus(y, dy)) for dc, dy in group]
    greet([by_rank(s) for s in (1, 2, 3, -1, -2, -3)] + peers)
    mine = c * 4 + y
    copies = []
    for d in range(1, WINDOW):
        for i, (src, dst) in enumerate(((k, kw), (v, vw), (doc_row, docw))):
            copies.append(
                remote(src, dst.at[WINDOW - 1 - d], halo_ss.at[d - 1, i], halo_rs.at[d - 1, i], by_rank(d))
            )
    halo = len(copies)
    for i, peer in enumerate(peers):
        copies.append(remote(meta, meta_out.at[mine], meta_ss.at[i], meta_rs.at[i], peer))
    for copy in copies:
        copy.start()
    meta_out[mine] = meta[...]
    kw[WINDOW - 1] = k[...]
    vw[WINDOW - 1] = v[...]
    docw[WINDOW - 1] = doc_row[...]
    for copy in copies[:halo]:
        copy.wait_recv()

    key_doc = jnp.concatenate([docw[i][0:1, :] for i in range(WINDOW)], 1)
    span = WINDOW * TOK
    key_pos = lax.broadcasted_iota(jnp.int32, (TOK, span), 1) + (rank - (WINDOW - 1)) * TOK
    query_pos = lax.broadcasted_iota(jnp.int32, (TOK, span), 0) + rank * TOK
    visible = (doc_col[...] == key_doc) & (key_pos <= query_pos) & (key_pos >= 0)
    square = jnp.zeros((TOK, 1), f32)
    for g in range(KV_HEADS):
        cols = slice(g * HEAD_DIM, (g + 1) * HEAD_DIM)
        keys = kw[:, :, cols].reshape(span, HEAD_DIM)
        values = vw[:, :, cols].reshape(span, HEAD_DIM)
        for h in range(GROUP):
            at = (g * GROUP + h) * HEAD_DIM
            here = slice(at, at + HEAD_DIM)
            scores = lax.dot_general(
                q[:, here], keys, (((1,), (1,)), ((), ())), preferred_element_type=f32
            ) * (HEAD_DIM ** -0.5)
            scores = jnp.where(visible, scores, masked_score)
            exps = jnp.exp(scores - jnp.max(scores, 1, keepdims=True))
            probs = (exps / jnp.sum(exps, 1, keepdims=True)).astype(bf16)
            context = jnp.dot(probs, values, preferred_element_type=f32).astype(bf16)
            resid = (hid[:, here].astype(f32) + context.astype(f32)).astype(bf16)
            resid_out[:, here] = resid
            resid_f = resid.astype(f32)
            square += jnp.sum(resid_f * resid_f, 1, keepdims=True)
    inverse = lax.rsqrt(square * (1.0 / D) + 1e-06)
    for n in range(NQ):
        cols = slice(n * CW, (n + 1) * CW)
        nrm_out[n] = (resid_out[:, cols].astype(f32) * inverse * gain[:, cols]).astype(bf16)
    for copy in copies[halo:]:
        copy.wait_recv()
    for copy in copies:
        copy.wait_send()


def find_slots(meta, slots, weights, c, y):
    s = lax.broadcasted_iota(jnp.int32, (16, TOPK, TOK), 0)
    expert = (((s >> 2) * 2 + c) * 8 + (s & 3) * 2 + (y >> 1)).astype(f32)
    earlier = lax.broadcasted_iota(jnp.int32, (TOK, TOK), 0) < lax.broadcasted_iota(
        jnp.int32, (TOK, TOK), 1
    )
    earlier = jnp.where(earlier, 1.0, 0.0).astype(bf16)
    for b in range(8):
        ids = meta[b][0:TOPK, :]
        hit = ids[None] == expert
        member = jnp.sum(jnp.where(hit, 1.0, 0.0), 1)
        before = jnp.dot(member.astype(bf16), earlier, preferred_element_type=f32)
        slots[:, b, :] = jnp.where(member > 0.5, before + float(CAP * b), -1.0)
        if weights is not None:
            weights[:, b, :] = jnp.sum(jnp.where(hit, meta[b][TOPK:, :][None], 0.0), 1)


def fill_places(slots, weights, out):
    def one(s, carry):
        rows = lax.broadcasted_iota(jnp.int32, (SLAB, TOK), 0).astype(f32)
        slot = slots[s]
        weight = None if weights is None else weights[s]
        for b in range(8):
            value = 1.0 if weight is None else weight[b : b + 1, :]
            out[s, :, b * TOK : (b + 1) * TOK] = jnp.where(
                rows == slot[b : b + 1, :], value, 0.0
            ).astype(bf16)
        return carry

    lax.fori_loop(0, 16, one, 0)


def expert_kernel(
    nrm, meta, wg_hbm, wu_hbm,
    inner_out, ma, mb, xa, xb,
    tok, places, slots, sa, sb, gate, up, wg, wu, xv,
    ay_ss, ay_rs, ac_ss, ac_rs, p1_ss, p1_rs, p2_ss, p2_rs, loc, wsem, lsem,
):
    x, c, z, y = coords()
    core = place(x, 1 - c, z, y)
    ypeer = [place(x, c, z, plus(y, d)) for d in range(1, 4)]
    xpeer = [place(plus(x, d), c, z, y) for d in range(1, 4)]
    zpeer = [place(x, c, plus(z, d), y) for d in range(1, 4)]
    greet([core] + ypeer + xpeer + zpeer)
    mine = c * 4 + y

    def ay(n, d):
        return remote(nrm.at[n], tok.at[n, mine], ay_ss.at[n, d - 1], ay_rs.at[n, d - 1], ypeer[d - 1])

    def ac(n, d):
        if d == 0:
            src = nrm.at[n]
            at = mine
        else:
            at = c * 4 + plus(y, 4 - d)
            src = tok.at[n, at]
        return remote(src, tok.at[n, at], ac_ss.at[n, d], ac_rs.at[n, d], core)

    def p1(n, buf, d):
        xp, zp = plus(x, d), plus(z, d)
        return (
            remote(sa.at[buf, xp], ma.at[n, :, x], p1_ss.at[n, 0, d - 1], p1_rs.at[n, 0, d - 1], xpeer[d - 1]),
            remote(sb.at[buf, zp], mb.at[n, :, z], p1_ss.at[n, 1, d - 1], p1_rs.at[n, 1, d - 1], zpeer[d - 1]),
        )

    def own(n, buf):
        return (
            pltpu.make_async_copy(sa.at[buf, x], ma.at[n, :, x], loc.at[n, 0]),
            pltpu.make_async_copy(sb.at[buf, z], mb.at[n, :, z], loc.at[n, 1]),
        )

    def p2(n, d):
        xp, zp = plus(x, d), plus(z, d)
        return (
            remote(ma.at[n, zp], xa.at[n, z], p2_ss.at[n, 0, d - 1], p2_rs.at[n, 0, d - 1], zpeer[d - 1]),
            remote(mb.at[n, xp], xb.at[n, x], p2_ss.at[n, 1, d - 1], p2_rs.at[n, 1, d - 1], xpeer[d - 1]),
        )

    weights = [
        pltpu.make_async_copy(wg_hbm, wg, wsem.at[0]),
        pltpu.make_async_copy(wu_hbm, wu, wsem.at[1]),
    ]
    for copy in weights:
        copy.start()

    def start_gather(n, carry):
        for d in range(1, 4):
            ay(n, d).start()
        ac(n, 0).start()
        tok[n, mine] = nrm[n]
        return carry

    lax.fori_loop(0, NQ, start_gather, 0)

    def forward(n):
        for d in range(1, 4):
            ay(n, d).wait_recv()
            ac(n, d).start()

    find_slots(meta, slots, None, c, y)
    fill_places(slots, None, places)
    forward(0)
    gate[...] = jnp.zeros_like(gate)
    up[...] = jnp.zeros_like(up)
    for copy in weights:
        copy.wait()

    def step(n, carry):
        @pl.when(n < NQ)
        def _():
            for d in range(4):
                ac(n, d).wait_recv()
            buf = lax.rem(n, NB)

            @pl.when(n >= NB)
            def _():
                for d in range(1, 4):
                    for copy in p1(n - NB, buf, d):
                        copy.wait_send()

            chunk = tok[n].reshape(8 * TOK, CW)
            for xp in range(4):
                rows = places[xp * 4 : xp * 4 + 4].reshape(4 * SLAB, 8 * TOK)
                packed = jnp.dot(rows, chunk, preferred_element_type=f32).astype(bf16)
                packed = packed.reshape(4, SLAB, CW)
                sa[buf, xp] = packed[:, :, :HW]
                sb[buf, :, xp] = packed[:, :, HW:]
            for d in range(1, 4):
                for copy in p1(n, buf, d):
                    copy.start()
            for copy in own(n, buf):
                copy.start()

            @pl.when(n + 1 < NQ)
            def _():
                forward(n + 1)

        @pl.when((n >= 1) & (n <= NQ))
        def _():
            for d in range(1, 4):
                for copy in p1(n - 1, 0, d):
                    copy.wait_recv()
            for copy in own(n - 1, 0):
                copy.wait()
            for d in range(1, 4):
                for copy in p2(n - 1, d):
                    copy.start()

        @pl.when(n >= 2)
        def _():
            m = n - 2
            loads = [
                pltpu.make_async_copy(ma.at[m, z], xv.at[z, :, :, 0:HW], lsem.at[0]),
                pltpu.make_async_copy(mb.at[m, x], xv.at[:, x, :, HW:CW], lsem.at[1]),
            ]
            for load in loads:
                load.start()
            for d in range(1, 4):
                for copy in p2(m, d):
                    copy.wait_recv()
                zs, xs = plus(z, 4 - d), plus(x, 4 - d)
                more = [
                    pltpu.make_async_copy(xa.at[m, zs], xv.at[zs, :, :, 0:HW], lsem.at[2 * d]),
                    pltpu.make_async_copy(xb.at[m, xs], xv.at[:, xs, :, HW:CW], lsem.at[2 * d + 1]),
                ]
                for load in more:
                    load.start()
                loads += more
            for load in loads:
                load.wait()
            for i in range(4):
                rows = xv[i].reshape(4 * SLAB, CW)
                gate[i] += jnp.dot(rows, wg[m], preferred_element_type=f32)
                up[i] += jnp.dot(rows, wu[m], preferred_element_type=f32)

        return carry

    lax.fori_loop(0, NQ + 2, step, 0)
    for i in range(4):
        value = gate[i]
        inner_out[i] = (value / (1.0 + jnp.exp(-value)) * up[i]).astype(bf16)

    def finish(n, carry):
        for d in range(1, 4):
            ay(n, d).wait_send()
            for copy in p2(n, d):
                copy.wait_send()
        for d in range(4):
            ac(n, d).wait_send()
        return carry

    lax.fori_loop(0, NQ, finish, 0)
    for n in range(NQ - NB, NQ):
        for d in range(1, 4):
            for copy in p1(n, n % NB, d):
                copy.wait_send()


def return_kernel(
    inner, meta, resid, wd_hbm,
    out, ra, rb, ya, yb,
    places, slots, weights, sr, wd, rv, total, half, core_in, mix, y_in,
    p1_ss, p1_rs, p2_ss, p2_rs, rc_ss, rc_rs, ry_ss, ry_rs, loc, wsem, lsem,
):
    x, c, z, y = coords()
    core = place(x, 1 - c, z, y)
    ypeer = [place(x, c, z, plus(y, d)) for d in range(1, 4)]
    xpeer = [place(plus(x, d), c, z, y) for d in range(1, 4)]
    zpeer = [place(x, c, plus(z, d), y) for d in range(1, 4)]
    load_wd = pltpu.make_async_copy(wd_hbm, wd, wsem)
    load_wd.start()
    greet([core] + ypeer + xpeer + zpeer)

    def p1(n, buf, d):
        xp, zp = plus(x, d), plus(z, d)
        return (
            remote(sr.at[buf, zp, :, :, 0:HW], ra.at[n, :, z], p1_ss.at[n, 0, d - 1], p1_rs.at[n, 0, d - 1], zpeer[d - 1]),
            remote(sr.at[buf, :, xp, :, HW:CW], rb.at[n, :, x], p1_ss.at[n, 1, d - 1], p1_rs.at[n, 1, d - 1], xpeer[d - 1]),
        )

    def own(n, buf):
        return (
            pltpu.make_async_copy(sr.at[buf, z, :, :, 0:HW], ra.at[n, :, z], loc.at[n, 0]),
            pltpu.make_async_copy(sr.at[buf, :, x, :, HW:CW], rb.at[n, :, x], loc.at[n, 1]),
        )

    def p2(n, d):
        xp, zp = plus(x, d), plus(z, d)
        return (
            remote(ra.at[n, xp], ya.at[n, x], p2_ss.at[n, 0, d - 1], p2_rs.at[n, 0, d - 1], xpeer[d - 1]),
            remote(rb.at[n, zp], yb.at[n, z], p2_ss.at[n, 1, d - 1], p2_rs.at[n, 1, d - 1], zpeer[d - 1]),
        )

    def rc(n):
        return remote(
            half.at[lax.rem(n, 2), 1 - c], core_in.at[n], rc_ss.at[n], rc_rs.at[n], core
        )

    def ry(n, d):
        return remote(
            mix.at[lax.rem(n, 2), plus(y, d)], y_in.at[n, d - 1], ry_ss.at[n, d - 1], ry_rs.at[n, d - 1], ypeer[d - 1]
        )

    load_wd.wait()

    def step(n, carry):
        @pl.when(n < NQ)
        def _():
            buf = lax.rem(n, NB)

            @pl.when(n >= NB)
            def _():
                for d in range(1, 4):
                    for copy in p1(n - NB, buf, d):
                        copy.wait_send()

            down = wd[:, pl.ds(pl.multiple_of(n * CW, CW), CW)]
            for i in range(4):
                part = jnp.dot(inner[i], down, preferred_element_type=f32).astype(bf16)
                sr[buf, i] = part.reshape(4, SLAB, CW)
            for d in range(1, 4):
                for copy in p1(n, buf, d):
                    copy.start()
            for copy in own(n, buf):
                copy.start()

        @pl.when(n == 0)
        def _():
            find_slots(meta, slots, weights, c, y)
            fill_places(slots, weights, places)

        @pl.when((n >= 1) & (n <= NQ))
        def _():
            for d in range(1, 4):
                for copy in p1(n - 1, 0, d):
                    copy.wait_recv()
            for copy in own(n - 1, 0):
                copy.wait()
            for d in range(1, 4):
                for copy in p2(n - 1, d):
                    copy.start()

        @pl.when((n >= 2) & (n <= NQ + 1))
        def _():
            m = n - 2
            loads = [
                pltpu.make_async_copy(ra.at[m, x], rv.at[x, :, :, 0:HW], lsem.at[0]),
                pltpu.make_async_copy(rb.at[m, z], rv.at[:, z, :, HW:CW], lsem.at[1]),
            ]
            for load in loads:
                load.start()
            for d in range(1, 4):
                for copy in p2(m, d):
                    copy.wait_recv()
                zs, xs = plus(z, 4 - d), plus(x, 4 - d)
                more = [
                    pltpu.make_async_copy(ya.at[m, xs], rv.at[xs, :, :, 0:HW], lsem.at[2 * d]),
                    pltpu.make_async_copy(yb.at[m, zs], rv.at[:, zs, :, HW:CW], lsem.at[2 * d + 1]),
                ]
                for load in more:
                    load.start()
                loads += more
            for load in loads:
                load.wait()
            moe = lax.dot_general(
                places[...].reshape(16 * SLAB, 8 * TOK),
                rv[...].reshape(16 * SLAB, CW),
                (((0,), (0,)), ((), ())),
                preferred_element_type=f32,
            )
            total[lax.rem(m, 2)] = moe.reshape(2, 4, TOK, CW)

            @pl.when(m >= 2)
            def _():
                rc(m - 2).wait_send()

            half[lax.rem(m, 2)] = total[lax.rem(m, 2)].astype(bf16)
            rc(m).start()

        @pl.when((n >= 3) & (n <= NQ + 2))
        def _():
            m = n - 3
            rc(m).wait_recv()

            @pl.when(m >= 2)
            def _():
                for d in range(1, 4):
                    ry(m - 2, d).wait_send()

            mix[lax.rem(m, 2)] = (total[lax.rem(m, 2), c] + core_in[m].astype(f32)).astype(bf16)
            for d in range(1, 4):
                ry(m, d).start()

        @pl.when(n >= 4)
        def _():
            m = n - 4
            value = mix[lax.rem(m, 2), y].astype(f32)
            for d in range(1, 4):
                ry(m, d).wait_recv()
                value += y_in[m, d - 1].astype(f32)
            cols = pl.ds(pl.multiple_of(m * CW, CW), CW)
            out[:, cols] = (resid[:, cols].astype(f32) + value).astype(bf16)

        return carry

    lax.fori_loop(0, NQ + 4, step, 0)

    def finish(n, carry):
        for d in range(1, 4):
            for copy in p2(n, d):
                copy.wait_send()
        return carry

    lax.fori_loop(0, NQ, finish, 0)
    for n in range(NQ - NB, NQ):
        for d in range(1, 4):
            for copy in p1(n, n % NB, d):
                copy.wait_send()
    for n in range(NQ - 2, NQ):
        rc(n).wait_send()
        for d in range(1, 4):
            ry(n, d).wait_send()


VM = pl.BlockSpec(memory_space=pltpu.VMEM)
ANY = pl.BlockSpec(memory_space=pl.ANY)


def dma(*shape):
    return pltpu.SemaphoreType.DMA(shape)


def params(collective_id):
    return pltpu.CompilerParams(
        collective_id=collective_id, has_side_effects=True, vmem_limit_bytes=62 << 20
    )


def on_device(
    hidden_in, queries, key_rows, value_rows, document_ids, norm_gain,
    w_gate, w_up, w_down, expert_ids, route_weights,
):
    docs = document_ids.astype(f32)
    doc_row = jnp.broadcast_to(docs[None, :], (8, TOK))
    meta = jnp.concatenate([expert_ids.T.astype(f32), route_weights.T], 0)
    resid, nrm, meta_all = pl.pallas_call(
        attend_kernel,
        out_shape=(
            jax.ShapeDtypeStruct((TOK, D), bf16),
            jax.ShapeDtypeStruct((NQ, TOK, CW), bf16),
            jax.ShapeDtypeStruct((8, 2 * TOPK, TOK), f32),
        ),
        in_specs=[VM] * 8,
        out_specs=(VM, VM, VM),
        scratch_shapes=[
            pltpu.VMEM((WINDOW, TOK, KV_HEADS * HEAD_DIM), bf16),
            pltpu.VMEM((WINDOW, TOK, KV_HEADS * HEAD_DIM), bf16),
            pltpu.VMEM((WINDOW, 8, TOK), f32),
            dma(3, 3), dma(3, 3), dma(7), dma(7),
        ],
        compiler_params=params(0),
    )(hidden_in, queries, key_rows, value_rows, doc_row, docs[:, None], meta, norm_gain[None, :])

    landing = jax.ShapeDtypeStruct((NQ, 4, 4, SLAB, HW), bf16)
    inner, *_ = pl.pallas_call(
        expert_kernel,
        out_shape=(jax.ShapeDtypeStruct((4, 4 * SLAB, FF_HALF), bf16),) + (landing,) * 4,
        in_specs=[VM, VM, ANY, ANY],
        out_specs=(VM,) + (ANY,) * 4,
        scratch_shapes=[
            pltpu.VMEM((NQ, 8, TOK, CW), bf16),
            pltpu.VMEM((16, SLAB, 8 * TOK), bf16),
            pltpu.VMEM((16, 8, TOK), f32),
            pltpu.VMEM((NB, 4, 4, SLAB, HW), bf16),
            pltpu.VMEM((NB, 4, 4, SLAB, HW), bf16),
            pltpu.VMEM((4, 4 * SLAB, FF_HALF), f32),
            pltpu.VMEM((4, 4 * SLAB, FF_HALF), f32),
            pltpu.VMEM((NQ, CW, FF_HALF), bf16),
            pltpu.VMEM((NQ, CW, FF_HALF), bf16),
            pltpu.VMEM((4, 4, SLAB, CW), bf16),
            dma(NQ, 3), dma(NQ, 3), dma(NQ, 4), dma(NQ, 4),
            dma(NQ, 2, 3), dma(NQ, 2, 3), dma(NQ, 2, 3), dma(NQ, 2, 3),
            dma(NQ, 2), dma(2), dma(8),
        ],
        compiler_params=params(1),
    )(nrm, meta_all, w_gate.reshape(NQ, CW, FF_HALF), w_up.reshape(NQ, CW, FF_HALF))

    out, *_ = pl.pallas_call(
        return_kernel,
        out_shape=(jax.ShapeDtypeStruct((TOK, D), bf16),) + (landing,) * 4,
        in_specs=[VM, VM, VM, ANY],
        out_specs=(VM,) + (ANY,) * 4,
        scratch_shapes=[
            pltpu.VMEM((16, SLAB, 8 * TOK), bf16),
            pltpu.VMEM((16, 8, TOK), f32),
            pltpu.VMEM((16, 8, TOK), f32),
            pltpu.VMEM((NB, 4, 4, SLAB, CW), bf16),
            pltpu.VMEM((FF_HALF, D), bf16),
            pltpu.VMEM((4, 4, SLAB, CW), bf16),
            pltpu.VMEM((2, 2, 4, TOK, CW), f32),
            pltpu.VMEM((2, 2, 4, TOK, CW), bf16),
            pltpu.VMEM((NQ, 4, TOK, CW), bf16),
            pltpu.VMEM((2, 4, TOK, CW), bf16),
            pltpu.VMEM((NQ, 3, TOK, CW), bf16),
            dma(NQ, 2, 3), dma(NQ, 2, 3), dma(NQ, 2, 3), dma(NQ, 2, 3),
            dma(NQ), dma(NQ), dma(NQ, 3), dma(NQ, 3),
            dma(NQ, 2), pltpu.SemaphoreType.DMA, dma(8),
        ],
        compiler_params=params(2),
    )(inner, meta_all, resid, w_down.reshape(FF_HALF, D))
    return out


def solution(mesh):
    rows = P(("ctx", "exp"), None)
    whole = P(("ctx", "exp"), None, None)
    in_specs = (
        rows, rows, rows, rows, P(("ctx", "exp")), P(), whole, whole, whole, rows, rows,
    )
    return jax.shard_map(
        on_device, mesh=mesh, in_specs=in_specs, out_specs=rows, check_vma=False
    )
```

```python
import jax
import jax.numpy as jnp
from jax import lax
from jax.experimental import pallas as pl
from jax.experimental.pallas import tpu as pltpu
from jax.sharding import PartitionSpec as P

D = 3584
KV_HEADS = 4
HEAD_DIM = 128
TOPK = 8
WINDOW = 4
GROUP = 7
TOK = 128
CAP = 17
FF_HALF = 640
NQ = 7
CW = D // NQ
HW = CW // 2
SLAB = 144
NB = 2
NF = 2
NS = NQ - NF

MESH = pl.DeviceIdType.MESH
masked_score = -1e30
bf16 = jnp.bfloat16
f32 = jnp.float32


def coords():
    ctx, ex = lax.axis_index("ctx"), lax.axis_index("exp")
    return ctx // 2, ctx % 2, ex // 4, ex % 4


def place(x, c, z, y):
    return (x * 2 + c, z * 4 + y)


def greet(partners):
    barrier = pltpu.get_barrier_semaphore()
    for partner in partners:
        pl.semaphore_signal(barrier, inc=1, device_id=partner, device_id_type=MESH)
    pl.semaphore_wait(barrier, len(partners))


def remote(src, dst, send_sem, recv_sem, device):
    return pltpu.make_async_remote_copy(
        src_ref=src,
        dst_ref=dst,
        send_sem=send_sem,
        recv_sem=recv_sem,
        device_id=device,
        device_id_type=MESH,
    )


def fetched(n, parity):
    return jnp.where(n < NF, 2 * n + parity, n + NF)


def plus(value, steps):
    return lax.rem(value + steps, 4)


def attend_kernel(
    hid, q, k, v, doc_row, doc_col, meta, gain,
    resid_out, nrm_out, meta_out,
    kw, vw, docw, halo_ss, halo_rs, meta_ss, meta_rs,
):
    x, c, z, y = coords()
    rank = lax.axis_index("ctx") * 16 + lax.axis_index("exp")

    def by_rank(steps):
        other = lax.rem(rank + steps + 128, 128)
        return (other // 16, lax.rem(other, 16))

    group = [(dc, dy) for dc in range(2) for dy in range(4) if (dc, dy) != (0, 0)]
    peers = [place(x, lax.rem(c + dc, 2), z, plus(y, dy)) for dc, dy in group]
    greet([by_rank(s) for s in (1, 2, 3, -1, -2, -3)] + peers)
    mine = c * 4 + y
    copies = []
    for d in range(1, WINDOW):
        for i, (src, dst) in enumerate(((k, kw), (v, vw), (doc_row, docw))):
            copies.append(
                remote(src, dst.at[WINDOW - 1 - d], halo_ss.at[d - 1, i], halo_rs.at[d - 1, i], by_rank(d))
            )
    halo = len(copies)
    for i, peer in enumerate(peers):
        copies.append(remote(meta, meta_out.at[mine], meta_ss.at[i], meta_rs.at[i], peer))
    for copy in copies:
        copy.start()
    meta_out[mine] = meta[...]
    kw[WINDOW - 1] = k[...]
    vw[WINDOW - 1] = v[...]
    docw[WINDOW - 1] = doc_row[...]
    for copy in copies[:halo]:
        copy.wait_recv()

    key_doc = jnp.concatenate([docw[i][0:1, :] for i in range(WINDOW)], 1)
    span = WINDOW * TOK
    key_pos = lax.broadcasted_iota(jnp.int32, (TOK, span), 1) + (rank - (WINDOW - 1)) * TOK
    query_pos = lax.broadcasted_iota(jnp.int32, (TOK, span), 0) + rank * TOK
    visible = (doc_col[...] == key_doc) & (key_pos <= query_pos) & (key_pos >= 0)
    square = jnp.zeros((TOK, 1), f32)
    for g in range(KV_HEADS):
        cols = slice(g * HEAD_DIM, (g + 1) * HEAD_DIM)
        keys = kw[:, :, cols].reshape(span, HEAD_DIM)
        values = vw[:, :, cols].reshape(span, HEAD_DIM)
        for h in range(GROUP):
            at = (g * GROUP + h) * HEAD_DIM
            here = slice(at, at + HEAD_DIM)
            scores = lax.dot_general(
                q[:, here], keys, (((1,), (1,)), ((), ())), preferred_element_type=f32
            ) * (HEAD_DIM ** -0.5)
            scores = jnp.where(visible, scores, masked_score)
            exps = jnp.exp(scores - jnp.max(scores, 1, keepdims=True))
            probs = (exps / jnp.sum(exps, 1, keepdims=True)).astype(bf16)
            context = jnp.dot(probs, values, preferred_element_type=f32).astype(bf16)
            resid = (hid[:, here].astype(f32) + context.astype(f32)).astype(bf16)
            resid_out[:, here] = resid
            resid_f = resid.astype(f32)
            square += jnp.sum(resid_f * resid_f, 1, keepdims=True)
    inverse = lax.rsqrt(square * (1.0 / D) + 1e-06)
    for n in range(NQ):
        cols = slice(n * CW, (n + 1) * CW)
        nrm_out[n] = (resid_out[:, cols].astype(f32) * inverse * gain[:, cols]).astype(bf16)
    for copy in copies[halo:]:
        copy.wait_recv()
    for copy in copies:
        copy.wait_send()


def find_slots(meta, slots, weights, c, y):
    s = lax.broadcasted_iota(jnp.int32, (16, TOPK, TOK), 0)
    expert = (((s >> 2) * 2 + c) * 8 + (s & 3) * 2 + (y >> 1)).astype(f32)
    earlier = lax.broadcasted_iota(jnp.int32, (TOK, TOK), 0) < lax.broadcasted_iota(
        jnp.int32, (TOK, TOK), 1
    )
    earlier = jnp.where(earlier, 1.0, 0.0).astype(bf16)
    for b in range(8):
        ids = meta[b][0:TOPK, :]
        hit = ids[None] == expert
        member = jnp.sum(jnp.where(hit, 1.0, 0.0), 1)
        before = jnp.dot(member.astype(bf16), earlier, preferred_element_type=f32)
        slots[:, b, :] = jnp.where(member > 0.5, before + float(CAP * b), -1.0)
        if weights is not None:
            weights[:, b, :] = jnp.sum(jnp.where(hit, meta[b][TOPK:, :][None], 0.0), 1)


def fill_places(slots, weights, out):
    def one(s, carry):
        rows = lax.broadcasted_iota(jnp.int32, (SLAB, TOK), 0).astype(f32)
        slot = slots[s]
        weight = None if weights is None else weights[s]
        for b in range(8):
            value = 1.0 if weight is None else weight[b : b + 1, :]
            out[s, :, b * TOK : (b + 1) * TOK] = jnp.where(
                rows == slot[b : b + 1, :], value, 0.0
            ).astype(bf16)
        return carry

    lax.fori_loop(0, 16, one, 0)


def expert_kernel(
    nrm, meta, wg_hbm, wu_hbm,
    inner_out, ma, mb, xa, xb, pa, pb,
    tok, places, slots, sa, sb, gate, up, wg, wu, xv,
    ay_ss, ay_rs, ac_ss, ac_rs, p1_ss, p1_rs, p2_ss, p2_rs, sw_ss, sw_rs, loc, wsem, lsem,
):
    x, c, z, y = coords()
    core = place(x, 1 - c, z, y)
    ypeer = [place(x, c, z, plus(y, d)) for d in range(1, 4)]
    xpeer = [place(plus(x, d), c, z, y) for d in range(1, 4)]
    zpeer = [place(x, c, plus(z, d), y) for d in range(1, 4)]
    greet([core] + ypeer + xpeer + zpeer)
    mine = c * 4 + y
    parity = lax.rem(y, 2)
    pair = place(x, c, z, y + 1 - 2 * parity)

    def ay(n, d):
        src = nrm.at[fetched(n, lax.rem(y + d, 2))]
        return remote(src, tok.at[n, mine], ay_ss.at[n, d - 1], ay_rs.at[n, d - 1], ypeer[d - 1])

    def ac(n, d):
        if d == 0:
            src = nrm.at[fetched(n, parity)]
            at = mine
        else:
            at = c * 4 + plus(y, 4 - d)
            src = tok.at[n, at]
        return remote(src, tok.at[n, at], ac_ss.at[n, d], ac_rs.at[n, d], core)

    def p1(n, buf, d):
        xp, zp = plus(x, d), plus(z, d)
        return (
            remote(sa.at[buf, xp], ma.at[n, :, x], p1_ss.at[n, 0, d - 1], p1_rs.at[n, 0, d - 1], xpeer[d - 1]),
            remote(sb.at[buf, zp], mb.at[n, :, z], p1_ss.at[n, 1, d - 1], p1_rs.at[n, 1, d - 1], zpeer[d - 1]),
        )

    def own(n, buf):
        return (
            pltpu.make_async_copy(sa.at[buf, x], ma.at[n, :, x], loc.at[n, 0]),
            pltpu.make_async_copy(sb.at[buf, z], mb.at[n, :, z], loc.at[n, 1]),
        )

    def p2(n, d):
        xp, zp = plus(x, d), plus(z, d)
        return (
            remote(ma.at[n, zp], xa.at[n, z], p2_ss.at[n, 0, d - 1], p2_rs.at[n, 0, d - 1], zpeer[d - 1]),
            remote(mb.at[n, xp], xb.at[n, x], p2_ss.at[n, 1, d - 1], p2_rs.at[n, 1, d - 1], xpeer[d - 1]),
        )

    def swap(n, d):
        zs, xs = plus(z, 4 - d), plus(x, 4 - d)
        a, b = (ma.at[n, z], mb.at[n, x]) if d == 0 else (xa.at[n, zs], xb.at[n, xs])
        return (
            remote(a, pa.at[n, zs], sw_ss.at[n, 0, d], sw_rs.at[n, 0, d], pair),
            remote(b, pb.at[n, xs], sw_ss.at[n, 1, d], sw_rs.at[n, 1, d], pair),
        )

    weights = [
        pltpu.make_async_copy(wg_hbm, wg, wsem.at[0]),
        pltpu.make_async_copy(wu_hbm, wu, wsem.at[1]),
    ]
    for copy in weights:
        copy.start()

    def start_gather(n, carry):
        for d in range(1, 4):
            ay(n, d).start()
        ac(n, 0).start()
        tok[n, mine] = nrm[fetched(n, parity)]
        return carry

    lax.fori_loop(0, NS, start_gather, 0)

    def forward(n):
        for d in range(1, 4):
            ay(n, d).wait_recv()
            ac(n, d).start()

    find_slots(meta, slots, None, c, y)
    fill_places(slots, None, places)
    forward(0)
    gate[...] = jnp.zeros_like(gate)
    up[...] = jnp.zeros_like(up)
    for copy in weights:
        copy.wait()

    def step(n, carry):
        @pl.when(n < NS)
        def _():
            for d in range(4):
                ac(n, d).wait_recv()
            buf = lax.rem(n, NB)

            @pl.when(n >= NB)
            def _():
                for d in range(1, 4):
                    for copy in p1(n - NB, buf, d):
                        copy.wait_send()

            chunk = tok[n].reshape(8 * TOK, CW)
            for xp in range(4):
                rows = places[xp * 4 : xp * 4 + 4].reshape(4 * SLAB, 8 * TOK)
                packed = jnp.dot(rows, chunk, preferred_element_type=f32).astype(bf16)
                packed = packed.reshape(4, SLAB, CW)
                sa[buf, xp] = packed[:, :, :HW]
                sb[buf, :, xp] = packed[:, :, HW:]
            for d in range(1, 4):
                for copy in p1(n, buf, d):
                    copy.start()
            for copy in own(n, buf):
                copy.start()

            @pl.when(n + 1 < NS)
            def _():
                forward(n + 1)

        @pl.when((n >= 1) & (n <= NS))
        def _():
            for d in range(1, 4):
                for copy in p1(n - 1, 0, d):
                    copy.wait_recv()
            for copy in own(n - 1, 0):
                copy.wait()
            for d in range(1, 4):
                for copy in p2(n - 1, d):
                    copy.start()

            @pl.when(n - 1 < NF)
            def _():
                for copy in swap(n - 1, 0):
                    copy.start()

        @pl.when(n >= 2)
        def _():
            m = n - 2
            swapped = (m == NS - 1) | (m == NS + 1)
            first = pltpu.make_async_copy

            @pl.when(jnp.logical_not(swapped))
            def _():
                i = jnp.minimum(m, NS - 1)
                loads = [
                    first(ma.at[i, z], xv.at[z, :, :, 0:HW], lsem.at[0]),
                    first(mb.at[i, x], xv.at[:, x, :, HW:CW], lsem.at[1]),
                ]
                for load in loads:
                    load.start()
                for d in range(1, 4):
                    for copy in p2(i, d):
                        copy.wait_recv()

                    @pl.when(i < NF)
                    def _():
                        for copy in swap(i, d):
                            copy.start()

                    zs, xs = plus(z, 4 - d), plus(x, 4 - d)
                    more = [
                        first(xa.at[i, zs], xv.at[zs, :, :, 0:HW], lsem.at[2 * d]),
                        first(xb.at[i, xs], xv.at[:, xs, :, HW:CW], lsem.at[2 * d + 1]),
                    ]
                    for load in more:
                        load.start()
                    loads += more
                for load in loads:
                    load.wait()

            @pl.when(swapped)
            def _():
                i = (m - NS + 1) // 2
                for d in range(4):
                    for copy in swap(i, d):
                        copy.wait_recv()
                loads = []
                for d in range(4):
                    loads += [
                        first(pa.at[i, d], xv.at[d, :, :, 0:HW], lsem.at[2 * d]),
                        first(pb.at[i, d], xv.at[:, d, :, HW:CW], lsem.at[2 * d + 1]),
                    ]
                for load in loads:
                    load.start()
                for load in loads:
                    load.wait()

            i = jnp.where(swapped, (m - NS + 1) // 2, jnp.minimum(m, NS - 1))
            chunk = fetched(i, jnp.where(swapped, 1 - parity, parity))
            for i in range(4):
                rows = xv[i].reshape(4 * SLAB, CW)
                gate[i] += jnp.dot(rows, wg[chunk], preferred_element_type=f32)
                up[i] += jnp.dot(rows, wu[chunk], preferred_element_type=f32)

        return carry

    lax.fori_loop(0, NQ + 2, step, 0)
    for i in range(4):
        value = gate[i]
        inner_out[i] = (value / (1.0 + jnp.exp(-value)) * up[i]).astype(bf16)

    def finish(n, carry):
        for d in range(1, 4):
            ay(n, d).wait_send()
            for copy in p2(n, d):
                copy.wait_send()
        for d in range(4):
            ac(n, d).wait_send()
        return carry

    lax.fori_loop(0, NS, finish, 0)
    for n in range(NF):
        for d in range(4):
            for copy in swap(n, d):
                copy.wait_send()
    for n in range(NS - NB, NS):
        for d in range(1, 4):
            for copy in p1(n, n % NB, d):
                copy.wait_send()


def return_kernel(
    inner, meta, resid, wd_hbm,
    out, ra, rb, ya, yb,
    places, slots, weights, sr, sw_out, sw_in, wd, rv, total, half, core_in, mix, y_in,
    p1_ss, p1_rs, p2_ss, p2_rs, rc_ss, rc_rs, ry_ss, ry_rs, sw_ss, sw_rs, loc, wsem, lsem,
):
    x, c, z, y = coords()
    core = place(x, 1 - c, z, y)
    ypeer = [place(x, c, z, plus(y, d)) for d in range(1, 4)]
    xpeer = [place(plus(x, d), c, z, y) for d in range(1, 4)]
    zpeer = [place(x, c, plus(z, d), y) for d in range(1, 4)]
    load_wd = pltpu.make_async_copy(wd_hbm, wd, wsem)
    load_wd.start()
    greet([core] + ypeer + xpeer + zpeer)

    def p1(n, buf, d):
        xp, zp = plus(x, d), plus(z, d)
        return (
            remote(sr.at[buf, zp, :, :, 0:HW], ra.at[n, :, z], p1_ss.at[n, 0, d - 1], p1_rs.at[n, 0, d - 1], zpeer[d - 1]),
            remote(sr.at[buf, :, xp, :, HW:CW], rb.at[n, :, x], p1_ss.at[n, 1, d - 1], p1_rs.at[n, 1, d - 1], xpeer[d - 1]),
        )

    def own(n, buf):
        return (
            pltpu.make_async_copy(sr.at[buf, z, :, :, 0:HW], ra.at[n, :, z], loc.at[n, 0]),
            pltpu.make_async_copy(sr.at[buf, :, x, :, HW:CW], rb.at[n, :, x], loc.at[n, 1]),
        )

    def p2(n, d):
        xp, zp = plus(x, d), plus(z, d)
        return (
            remote(ra.at[n, xp], ya.at[n, x], p2_ss.at[n, 0, d - 1], p2_rs.at[n, 0, d - 1], xpeer[d - 1]),
            remote(rb.at[n, zp], yb.at[n, z], p2_ss.at[n, 1, d - 1], p2_rs.at[n, 1, d - 1], zpeer[d - 1]),
        )

    def rc(n):
        return remote(
            half.at[lax.rem(n, 2), 1 - c], core_in.at[n], rc_ss.at[n], rc_rs.at[n], core
        )

    def ry(n, d):
        return remote(
            mix.at[lax.rem(n, 2), plus(y, d)], y_in.at[n, d - 1], ry_ss.at[n, d - 1], ry_rs.at[n, d - 1], ypeer[d - 1]
        )

    parity = lax.rem(y, 2)
    pair = place(x, c, z, y + 1 - 2 * parity)

    def swap(i):
        return remote(sw_out.at[i], sw_in.at[i], sw_ss.at[i], sw_rs.at[i], pair)

    def down(i, chunk):
        cols = pl.ds(pl.multiple_of(chunk * CW, CW), CW)
        return jnp.dot(inner[i], wd[:, cols], preferred_element_type=f32)

    def start_swap(n):
        for i in range(4):
            part = down(i, 2 * n + 1 - parity).astype(bf16)
            sw_out[n, i] = part.reshape(4, SLAB, CW)
        swap(n).start()

    load_wd.wait()
    start_swap(0)

    def step(n, carry):
        @pl.when(n < NS)
        def _():
            buf = lax.rem(n, NB)

            @pl.when(n >= NB)
            def _():
                for d in range(1, 4):
                    for copy in p1(n - NB, buf, d):
                        copy.wait_send()

            @pl.when(n < NS - NF)
            def _():
                for i in range(4):
                    part = down(i, 2 * NF + n)
                    sr[buf, i] = part.astype(bf16).reshape(4, SLAB, CW)

            @pl.when(n >= NS - NF)
            def _():
                at = n - (NS - NF)
                swap(at).wait_recv()
                for i in range(4):
                    part = down(i, 2 * at + parity).reshape(4, SLAB, CW)
                    sr[buf, i] = (part + sw_in[at, i].astype(f32)).astype(bf16)

            for d in range(1, 4):
                for copy in p1(n, buf, d):
                    copy.start()
            for copy in own(n, buf):
                copy.start()

        @pl.when(n == 0)
        def _():
            for i in range(1, NF):
                start_swap(i)
            find_slots(meta, slots, weights, c, y)
            fill_places(slots, weights, places)

        @pl.when((n >= 1) & (n <= NS))
        def _():
            for d in range(1, 4):
                for copy in p1(n - 1, 0, d):
                    copy.wait_recv()
            for copy in own(n - 1, 0):
                copy.wait()
            for d in range(1, 4):
                for copy in p2(n - 1, d):
                    copy.start()

        @pl.when((n >= 2) & (n <= NS + 1))
        def _():
            m = n - 2
            loads = [
                pltpu.make_async_copy(ra.at[m, x], rv.at[x, :, :, 0:HW], lsem.at[0]),
                pltpu.make_async_copy(rb.at[m, z], rv.at[:, z, :, HW:CW], lsem.at[1]),
            ]
            for load in loads:
                load.start()
            for d in range(1, 4):
                for copy in p2(m, d):
                    copy.wait_recv()
                zs, xs = plus(z, 4 - d), plus(x, 4 - d)
                more = [
                    pltpu.make_async_copy(ya.at[m, xs], rv.at[xs, :, :, 0:HW], lsem.at[2 * d]),
                    pltpu.make_async_copy(yb.at[m, zs], rv.at[:, zs, :, HW:CW], lsem.at[2 * d + 1]),
                ]
                for load in more:
                    load.start()
                loads += more
            for load in loads:
                load.wait()
            moe = lax.dot_general(
                places[...].reshape(16 * SLAB, 8 * TOK),
                rv[...].reshape(16 * SLAB, CW),
                (((0,), (0,)), ((), ())),
                preferred_element_type=f32,
            )
            total[lax.rem(m, 2)] = moe.reshape(2, 4, TOK, CW)

            @pl.when(m >= 2)
            def _():
                rc(m - 2).wait_send()

            half[lax.rem(m, 2)] = total[lax.rem(m, 2)].astype(bf16)
            rc(m).start()

        @pl.when((n >= 3) & (n <= NS + 2))
        def _():
            m = n - 3
            rc(m).wait_recv()

            @pl.when(m >= 2)
            def _():
                for d in range(1, 4):
                    ry(m - 2, d).wait_send()

            mix[lax.rem(m, 2)] = (total[lax.rem(m, 2), c] + core_in[m].astype(f32)).astype(bf16)
            for d in range(1, 4):
                ry(m, d).start()

        @pl.when(n >= 4)
        def _():
            m = n - 4
            for d in range(1, 4):
                ry(m, d).wait_recv()
            own_part = mix[lax.rem(m, 2), y].astype(f32)
            one, two, three = [y_in[m, i].astype(f32) for i in range(3)]

            def put(chunk, value):
                cols = pl.ds(pl.multiple_of(chunk * CW, CW), CW)
                out[:, cols] = (resid[:, cols].astype(f32) + value).astype(bf16)

            @pl.when(m < NS - NF)
            def _():
                put(2 * NF + m, own_part + one + two + three)

            @pl.when(m >= NS - NF)
            def _():
                at = 2 * (m - (NS - NF))
                put(at + parity, own_part + two)
                put(at + 1 - parity, one + three)

        return carry

    lax.fori_loop(0, NS + 4, step, 0)

    def finish(n, carry):
        for d in range(1, 4):
            for copy in p2(n, d):
                copy.wait_send()
        return carry

    lax.fori_loop(0, NS, finish, 0)
    for n in range(NS - NB, NS):
        for d in range(1, 4):
            for copy in p1(n, n % NB, d):
                copy.wait_send()
    for n in range(NS - 2, NS):
        rc(n).wait_send()
        for d in range(1, 4):
            ry(n, d).wait_send()
    for n in range(NF):
        swap(n).wait_send()


VM = pl.BlockSpec(memory_space=pltpu.VMEM)
ANY = pl.BlockSpec(memory_space=pl.ANY)


def dma(*shape):
    return pltpu.SemaphoreType.DMA(shape)


def params(collective_id):
    return pltpu.CompilerParams(
        collective_id=collective_id, has_side_effects=True, vmem_limit_bytes=62 << 20
    )


def on_device(
    hidden_in, queries, key_rows, value_rows, document_ids, norm_gain,
    w_gate, w_up, w_down, expert_ids, route_weights,
):
    docs = document_ids.astype(f32)
    doc_row = jnp.broadcast_to(docs[None, :], (8, TOK))
    meta = jnp.concatenate([expert_ids.T.astype(f32), route_weights.T], 0)
    resid, nrm, meta_all = pl.pallas_call(
        attend_kernel,
        out_shape=(
            jax.ShapeDtypeStruct((TOK, D), bf16),
            jax.ShapeDtypeStruct((NQ, TOK, CW), bf16),
            jax.ShapeDtypeStruct((8, 2 * TOPK, TOK), f32),
        ),
        in_specs=[VM] * 8,
        out_specs=(VM, VM, VM),
        scratch_shapes=[
            pltpu.VMEM((WINDOW, TOK, KV_HEADS * HEAD_DIM), bf16),
            pltpu.VMEM((WINDOW, TOK, KV_HEADS * HEAD_DIM), bf16),
            pltpu.VMEM((WINDOW, 8, TOK), f32),
            dma(3, 3), dma(3, 3), dma(7), dma(7),
        ],
        compiler_params=params(0),
    )(hidden_in, queries, key_rows, value_rows, doc_row, docs[:, None], meta, norm_gain[None, :])

    landing = jax.ShapeDtypeStruct((NS, 4, 4, SLAB, HW), bf16)
    swapped = jax.ShapeDtypeStruct((NF, 4, 4, SLAB, HW), bf16)
    inner, *_ = pl.pallas_call(
        expert_kernel,
        out_shape=(jax.ShapeDtypeStruct((4, 4 * SLAB, FF_HALF), bf16),) + (landing,) * 4 + (swapped,) * 2,
        in_specs=[VM, VM, ANY, ANY],
        out_specs=(VM,) + (ANY,) * 6,
        scratch_shapes=[
            pltpu.VMEM((NS, 8, TOK, CW), bf16),
            pltpu.VMEM((16, SLAB, 8 * TOK), bf16),
            pltpu.VMEM((16, 8, TOK), f32),
            pltpu.VMEM((NB, 4, 4, SLAB, HW), bf16),
            pltpu.VMEM((NB, 4, 4, SLAB, HW), bf16),
            pltpu.VMEM((4, 4 * SLAB, FF_HALF), f32),
            pltpu.VMEM((4, 4 * SLAB, FF_HALF), f32),
            pltpu.VMEM((NQ, CW, FF_HALF), bf16),
            pltpu.VMEM((NQ, CW, FF_HALF), bf16),
            pltpu.VMEM((4, 4, SLAB, CW), bf16),
            dma(NS, 3), dma(NS, 3), dma(NS, 4), dma(NS, 4),
            dma(NS, 2, 3), dma(NS, 2, 3), dma(NS, 2, 3), dma(NS, 2, 3),
            dma(NF, 2, 4), dma(NF, 2, 4), dma(NS, 2), dma(2), dma(8),
        ],
        compiler_params=params(1),
    )(nrm, meta_all, w_gate.reshape(NQ, CW, FF_HALF), w_up.reshape(NQ, CW, FF_HALF))

    out, *_ = pl.pallas_call(
        return_kernel,
        out_shape=(jax.ShapeDtypeStruct((TOK, D), bf16),) + (landing,) * 4,
        in_specs=[VM, VM, VM, ANY],
        out_specs=(VM,) + (ANY,) * 4,
        scratch_shapes=[
            pltpu.VMEM((16, SLAB, 8 * TOK), bf16),
            pltpu.VMEM((16, 8, TOK), f32),
            pltpu.VMEM((16, 8, TOK), f32),
            pltpu.VMEM((NB, 4, 4, SLAB, CW), bf16),
            pltpu.VMEM((NF, 4, 4, SLAB, CW), bf16),
            pltpu.VMEM((NF, 4, 4, SLAB, CW), bf16),
            pltpu.VMEM((FF_HALF, D), bf16),
            pltpu.VMEM((4, 4, SLAB, CW), bf16),
            pltpu.VMEM((2, 2, 4, TOK, CW), f32),
            pltpu.VMEM((2, 2, 4, TOK, CW), bf16),
            pltpu.VMEM((NS, 4, TOK, CW), bf16),
            pltpu.VMEM((2, 4, TOK, CW), bf16),
            pltpu.VMEM((NS, 3, TOK, CW), bf16),
            dma(NS, 2, 3), dma(NS, 2, 3), dma(NS, 2, 3), dma(NS, 2, 3),
            dma(NS), dma(NS), dma(NS, 3), dma(NS, 3),
            dma(NF), dma(NF), dma(NS, 2), pltpu.SemaphoreType.DMA, dma(8),
        ],
        compiler_params=params(2),
    )(inner, meta_all, resid, w_down.reshape(FF_HALF, D))
    return out


def solution(mesh):
    rows = P(("ctx", "exp"), None)
    whole = P(("ctx", "exp"), None, None)
    in_specs = (
        rows, rows, rows, rows, P(("ctx", "exp")), P(), whole, whole, whole, rows, rows,
    )
    return jax.shard_map(
        on_device, mesh=mesh, in_specs=in_specs, out_specs=rows, check_vma=False
    )
```

```python
import jax
import jax.numpy as jnp
from jax import lax
from jax.experimental import pallas as pl
from jax.experimental.pallas import tpu as pltpu
from jax.sharding import PartitionSpec as P

D = 3584
KV_HEADS = 4
HEAD_DIM = 128
TOPK = 8
WINDOW = 4
GROUP = 7
TOK = 128
CAP = 17
FF_HALF = 640
NQ = 7
CW = D // NQ
HW = CW // 2
SLAB = 144
OUT_AHEAD = 1
BACK_AHEAD = 2
NF = 2
NS = NQ - NF

MESH = pl.DeviceIdType.MESH
masked_score = -1e30
bf16 = jnp.bfloat16
f32 = jnp.float32


def coords():
    ctx, ex = lax.axis_index("ctx"), lax.axis_index("exp")
    return ctx // 2, ctx % 2, ex // 4, ex % 4


def place(x, c, z, y):
    return (x * 2 + c, z * 4 + y)


def greet(partners):
    barrier = pltpu.get_barrier_semaphore()
    for partner in partners:
        pl.semaphore_signal(barrier, inc=1, device_id=partner, device_id_type=MESH)
    pl.semaphore_wait(barrier, len(partners))


def remote(src, dst, send_sem, recv_sem, device):
    return pltpu.make_async_remote_copy(
        src_ref=src,
        dst_ref=dst,
        send_sem=send_sem,
        recv_sem=recv_sem,
        device_id=device,
        device_id_type=MESH,
    )


def fetched(n, parity):
    return jnp.where(n < NF, 2 * n + parity, n + NF)


def plus(value, steps):
    return lax.rem(value + steps, 4)


def attend(
    x, c, z, y, rank, hid, q, k, v, doc, ids, route, gain, resid_out, nrm, meta_all,
    kw, vw, docw, meta, halo_ss, halo_rs, doc_ss, doc_rs, meta_ss, meta_rs, by_rank, peers,
):
    mine = c * 4 + y
    row = jnp.broadcast_to(doc[...].astype(f32), (TOK, TOK))
    docw[WINDOW - 1] = row[0:8]
    meta[0:TOPK] = ids[...].astype(f32)
    meta[TOPK:] = route[...]

    def send_doc(d):
        return remote(
            docw.at[WINDOW - 1], docw.at[WINDOW - 1 - d], doc_ss.at[d - 1], doc_rs.at[d - 1], by_rank(d)
        )

    def send_head(g, d):
        cols = pl.ds(g * HEAD_DIM, HEAD_DIM)
        return [
            remote(
                src.at[:, cols], dst.at[g, WINDOW - 1 - d], halo_ss.at[g, d - 1, i], halo_rs.at[g, d - 1, i], by_rank(d)
            )
            for i, (src, dst) in enumerate(((k, kw), (v, vw)))
        ]

    def send_meta(i):
        return remote(meta, meta_all.at[mine], meta_ss.at[i], meta_rs.at[i], peers[i])

    for d in range(1, WINDOW):
        send_doc(d).start()
    for g in range(KV_HEADS):
        for d in range(1, WINDOW):
            for copy in send_head(g, d):
                copy.start()
    for i in range(7):
        send_meta(i).start()
    meta_all[mine] = meta[...]
    for g in range(KV_HEADS):
        cols = slice(g * HEAD_DIM, (g + 1) * HEAD_DIM)
        kw[g, WINDOW - 1] = k[:, cols]
        vw[g, WINDOW - 1] = v[:, cols]
    for d in range(1, WINDOW):
        send_doc(d).wait_recv()

    key_doc = jnp.concatenate([docw[i][0:1, :] for i in range(WINDOW)], 1)
    span = WINDOW * TOK
    column = row.T
    query_doc = jnp.concatenate([column] * WINDOW, 1)
    key_pos = lax.broadcasted_iota(jnp.int32, (TOK, span), 1) + (rank - (WINDOW - 1)) * TOK
    query_pos = lax.broadcasted_iota(jnp.int32, (TOK, span), 0) + rank * TOK
    visible = (query_doc == key_doc) & (key_pos <= query_pos) & (key_pos >= 0)
    square = jnp.zeros((TOK, 1), f32)
    for g in range(KV_HEADS):
        for d in range(1, WINDOW):
            for copy in send_head(g, d):
                copy.wait_recv()
        keys = kw[g].reshape(span, HEAD_DIM)
        values = vw[g].reshape(span, HEAD_DIM)
        for h in range(GROUP):
            at = (g * GROUP + h) * HEAD_DIM
            here = slice(at, at + HEAD_DIM)
            scores = lax.dot_general(
                q[:, here], keys, (((1,), (1,)), ((), ())), preferred_element_type=f32
            ) * (HEAD_DIM ** -0.5)
            scores = jnp.where(visible, scores, masked_score)
            exps = jnp.exp(scores - jnp.max(scores, 1, keepdims=True))
            probs = (exps / jnp.sum(exps, 1, keepdims=True)).astype(bf16)
            context = jnp.dot(probs, values, preferred_element_type=f32).astype(bf16)
            resid = (hid[:, here].astype(f32) + context.astype(f32)).astype(bf16)
            resid_out[:, here] = resid
            resid_f = resid.astype(f32)
            square += jnp.sum(resid_f * resid_f, 1, keepdims=True)
    inverse = lax.rsqrt(square * (1.0 / D) + 1e-06)
    for n in range(NQ):
        cols = slice(n * CW, (n + 1) * CW)
        nrm[n] = (resid_out[:, cols].astype(f32) * inverse * gain[:, cols]).astype(bf16)
    for i in range(7):
        send_meta(i).wait_recv()

    def finish():
        for d in range(1, WINDOW):
            send_doc(d).wait_send()
        for g in range(KV_HEADS):
            for d in range(1, WINDOW):
                for copy in send_head(g, d):
                    copy.wait_send()
        for i in range(7):
            send_meta(i).wait_send()

    return finish


def find_slots(meta, slots, weights, c, y):
    s = lax.broadcasted_iota(jnp.int32, (16, TOPK, TOK), 0)
    expert = (((s >> 2) * 2 + c) * 8 + (s & 3) * 2 + (y >> 1)).astype(f32)
    earlier = lax.broadcasted_iota(jnp.int32, (TOK, TOK), 0) < lax.broadcasted_iota(
        jnp.int32, (TOK, TOK), 1
    )
    earlier = jnp.where(earlier, 1.0, 0.0).astype(bf16)
    for b in range(8):
        ids = meta[b][0:TOPK, :]
        hit = ids[None] == expert
        member = jnp.sum(jnp.where(hit, 1.0, 0.0), 1)
        before = jnp.dot(member.astype(bf16), earlier, preferred_element_type=f32)
        slots[:, b, :] = jnp.where(member > 0.5, before + float(CAP * b), -1.0)
        if weights is not None:
            weights[:, b, :] = jnp.sum(jnp.where(hit, meta[b][TOPK:, :][None], 0.0), 1)


def fill_places(slots, weights, out):
    def one(s, carry):
        rows = lax.broadcasted_iota(jnp.int32, (SLAB, TOK), 0).astype(f32)
        slot = slots[s]
        weight = None if weights is None else weights[s]
        for b in range(8):
            value = 1.0 if weight is None else weight[b : b + 1, :]
            out[s, :, b * TOK : (b + 1) * TOK] = jnp.where(
                rows == slot[b : b + 1, :], value, 0.0
            ).astype(bf16)
        return carry

    lax.fori_loop(0, 16, one, 0)


def expert_kernel(
    hid, q, k, v, doc, ids, route, gain, wg_hbm, wu_hbm,
    resid_out, meta_all, inner_out, ma, mb, xa, xb, pa, pb,
    kw, vw, docw, meta, halo_ss, halo_rs, doc_ss, doc_rs, meta_ss, meta_rs, nrm, tok, places, slots, sa, sb, gate, up, wg, wu, xv,
    ay_ss, ay_rs, ac_ss, ac_rs, p1_ss, p1_rs, p2_ss, p2_rs, sw_ss, sw_rs, loc, wsem, lsem,
):
    x, c, z, y = coords()
    core = place(x, 1 - c, z, y)
    ypeer = [place(x, c, z, plus(y, d)) for d in range(1, 4)]
    xpeer = [place(plus(x, d), c, z, y) for d in range(1, 4)]
    zpeer = [place(x, c, plus(z, d), y) for d in range(1, 4)]
    rank = lax.axis_index("ctx") * 16 + lax.axis_index("exp")

    def by_rank(steps):
        other = lax.rem(rank + steps + 128, 128)
        return (other // 16, lax.rem(other, 16))

    peers = [core] + ypeer + [place(x, 1 - c, z, plus(y, d)) for d in range(1, 4)]
    weights = [
        pltpu.make_async_copy(wg_hbm, wg, wsem.at[0]),
        pltpu.make_async_copy(wu_hbm, wu, wsem.at[1]),
    ]
    for copy in weights:
        copy.start()

    greet([by_rank(d) for d in (1, 2, 3, -1, -2, -3)] + peers + xpeer + zpeer)
    finish_attend = attend(
        x, c, z, y, rank, hid, q, k, v, doc, ids, route, gain, resid_out, nrm, meta_all,
        kw, vw, docw, meta, halo_ss, halo_rs, doc_ss, doc_rs, meta_ss, meta_rs, by_rank, peers,
    )
    mine = c * 4 + y
    parity = lax.rem(y, 2)
    pair = place(x, c, z, y + 1 - 2 * parity)

    def ay(n, d):
        src = nrm.at[fetched(n, lax.rem(y + d, 2))]
        return remote(src, tok.at[n, mine], ay_ss.at[n, d - 1], ay_rs.at[n, d - 1], ypeer[d - 1])

    def ac(n, d):
        if d == 0:
            src = nrm.at[fetched(n, parity)]
            at = mine
        else:
            at = c * 4 + plus(y, 4 - d)
            src = tok.at[n, at]
        return remote(src, tok.at[n, at], ac_ss.at[n, d], ac_rs.at[n, d], core)

    def p1(n, d):
        xp, zp = plus(x, d), plus(z, d)
        return (
            remote(sa.at[n, xp], ma.at[n, :, x], p1_ss.at[n, 0, d - 1], p1_rs.at[n, 0, d - 1], xpeer[d - 1]),
            remote(sb.at[n, zp], mb.at[n, :, z], p1_ss.at[n, 1, d - 1], p1_rs.at[n, 1, d - 1], zpeer[d - 1]),
        )

    def own(n):
        return (
            pltpu.make_async_copy(sa.at[n, x], ma.at[n, :, x], loc.at[n, 0]),
            pltpu.make_async_copy(sb.at[n, z], mb.at[n, :, z], loc.at[n, 1]),
        )

    def p2(n, d):
        xp, zp = plus(x, d), plus(z, d)
        return (
            remote(ma.at[n, zp], xa.at[n, z], p2_ss.at[n, 0, d - 1], p2_rs.at[n, 0, d - 1], zpeer[d - 1]),
            remote(mb.at[n, xp], xb.at[n, x], p2_ss.at[n, 1, d - 1], p2_rs.at[n, 1, d - 1], xpeer[d - 1]),
        )

    def swap(n, d):
        zs, xs = plus(z, 4 - d), plus(x, 4 - d)
        a, b = (ma.at[n, z], mb.at[n, x]) if d == 0 else (xa.at[n, zs], xb.at[n, xs])
        return (
            remote(a, pa.at[n, zs], sw_ss.at[n, 0, d], sw_rs.at[n, 0, d], pair),
            remote(b, pb.at[n, xs], sw_ss.at[n, 1, d], sw_rs.at[n, 1, d], pair),
        )

    def start_gather(n):
        for d in range(1, 4):
            ay(n, d).start()
        ac(n, 0).start()
        tok[n, mine] = nrm[fetched(n, parity)]

    start_gather(0)

    def forward(n):
        for d in range(1, 4):
            ay(n, d).wait_recv()
            ac(n, d).start()

    find_slots(meta_all, slots, None, c, y)
    fill_places(slots, None, places)
    forward(0)
    start_gather(1)
    gate[...] = jnp.zeros_like(gate)
    up[...] = jnp.zeros_like(up)
    for copy in weights:
        copy.wait()

    def step(n, carry):
        @pl.when(n < NS)
        def _():
            for d in range(4):
                ac(n, d).wait_recv()
            chunk = tok[n].reshape(8 * TOK, CW)
            for xp in range(4):
                rows = places[xp * 4 : xp * 4 + 4].reshape(4 * SLAB, 8 * TOK)
                packed = jnp.dot(rows, chunk, preferred_element_type=f32).astype(bf16)
                packed = packed.reshape(4, SLAB, CW)
                sa[n, xp] = packed[:, :, :HW]
                sb[n, :, xp] = packed[:, :, HW:]
            for d in range(1, 4):
                for copy in p1(n, d):
                    copy.start()
            for copy in own(n):
                copy.start()

            @pl.when(n + 1 < NS)
            def _():
                forward(n + 1)

            @pl.when(n + 2 < NS)
            def _():
                start_gather(n + 2)

        @pl.when((n >= OUT_AHEAD) & (n < NS + OUT_AHEAD))
        def _():
            i = n - OUT_AHEAD
            for d in range(1, 4):
                for copy in p1(i, d):
                    copy.wait_recv()
            for copy in own(i):
                copy.wait()
            for d in range(1, 4):
                for copy in p2(i, d):
                    copy.start()

            @pl.when(i < NF)
            def _():
                for copy in swap(i, 0):
                    copy.start()

        @pl.when((n > OUT_AHEAD) & (n <= OUT_AHEAD + NF))
        def _():
            i = n - OUT_AHEAD - 1
            for d in range(1, 4):
                for copy in p2(i, d):
                    copy.wait_recv()
                for copy in swap(i, d):
                    copy.start()

        @pl.when(n >= OUT_AHEAD + 2)
        def _():
            m = n - OUT_AHEAD - 2
            swapped = (m == NS - 1) | (m == NS + 1)
            first = pltpu.make_async_copy

            @pl.when(jnp.logical_not(swapped))
            def _():
                i = jnp.minimum(m, NS - 1)
                loads = [
                    first(ma.at[i, z], xv.at[z, :, :, 0:HW], lsem.at[0]),
                    first(mb.at[i, x], xv.at[:, x, :, HW:CW], lsem.at[1]),
                ]
                for load in loads:
                    load.start()
                for d in range(1, 4):
                    @pl.when(i >= NF)
                    def _():
                        for copy in p2(i, d):
                            copy.wait_recv()

                    zs, xs = plus(z, 4 - d), plus(x, 4 - d)
                    more = [
                        first(xa.at[i, zs], xv.at[zs, :, :, 0:HW], lsem.at[2 * d]),
                        first(xb.at[i, xs], xv.at[:, xs, :, HW:CW], lsem.at[2 * d + 1]),
                    ]
                    for load in more:
                        load.start()
                    loads += more
                for load in loads:
                    load.wait()

            @pl.when(swapped)
            def _():
                i = (m - NS + 1) // 2
                for d in range(4):
                    for copy in swap(i, d):
                        copy.wait_recv()
                loads = []
                for d in range(4):
                    loads += [
                        first(pa.at[i, d], xv.at[d, :, :, 0:HW], lsem.at[2 * d]),
                        first(pb.at[i, d], xv.at[:, d, :, HW:CW], lsem.at[2 * d + 1]),
                    ]
                for load in loads:
                    load.start()
                for load in loads:
                    load.wait()

            i = jnp.where(swapped, (m - NS + 1) // 2, jnp.minimum(m, NS - 1))
            chunk = fetched(i, jnp.where(swapped, 1 - parity, parity))
            for i in range(4):
                rows = xv[i].reshape(4 * SLAB, CW)
                gate[i] += jnp.dot(rows, wg[chunk], preferred_element_type=f32)
                up[i] += jnp.dot(rows, wu[chunk], preferred_element_type=f32)

        return carry

    lax.fori_loop(0, NQ + OUT_AHEAD + 2, step, 0)
    for i in range(4):
        value = gate[i]
        inner_out[i] = (value / (1.0 + jnp.exp(-value)) * up[i]).astype(bf16)

    def finish(n, carry):
        for d in range(1, 4):
            ay(n, d).wait_send()
            for copy in p1(n, d) + p2(n, d):
                copy.wait_send()
        for d in range(4):
            ac(n, d).wait_send()
        return carry

    lax.fori_loop(0, NS, finish, 0)
    for n in range(NF):
        for d in range(4):
            for copy in swap(n, d):
                copy.wait_send()
    finish_attend()


def return_kernel(
    inner, meta, resid, wd_hbm,
    out, ra, rb, ya, yb,
    places, slots, weights, sr, sw_out, sw_in, wd, rv, total, half, core_in, mix, y_in,
    p1_ss, p1_rs, p2_ss, p2_rs, rc_ss, rc_rs, ry_ss, ry_rs, sw_ss, sw_rs, loc, wsem, lsem,
):
    x, c, z, y = coords()
    core = place(x, 1 - c, z, y)
    ypeer = [place(x, c, z, plus(y, d)) for d in range(1, 4)]
    xpeer = [place(plus(x, d), c, z, y) for d in range(1, 4)]
    zpeer = [place(x, c, plus(z, d), y) for d in range(1, 4)]
    load_wd = pltpu.make_async_copy(wd_hbm, wd, wsem)
    load_wd.start()
    greet([core] + ypeer + xpeer + zpeer)

    def p1_z(n, d):
        zp = plus(z, d)
        return remote(
            sr.at[n, zp, :, :, 0:HW], ra.at[n, :, z], p1_ss.at[n, 0, d - 1], p1_rs.at[n, 0, d - 1], zpeer[d - 1]
        )

    def p1(n, d):
        xp = plus(x, d)
        return (
            p1_z(n, d),
            remote(sr.at[n, :, xp, :, HW:CW], rb.at[n, :, x], p1_ss.at[n, 1, d - 1], p1_rs.at[n, 1, d - 1], xpeer[d - 1]),
        )

    def p1_part(n, i, d):
        xp = plus(x, d)
        return remote(
            sr.at[n, i, xp, :, HW:CW], rb.at[n, i, x], p1_ss.at[n, 1, d - 1], p1_rs.at[n, 1, d - 1], xpeer[d - 1]
        )

    def own(n):
        return (
            pltpu.make_async_copy(sr.at[n, z, :, :, 0:HW], ra.at[n, :, z], loc.at[n, 0]),
            pltpu.make_async_copy(sr.at[n, :, x, :, HW:CW], rb.at[n, :, x], loc.at[n, 1]),
        )

    def p2(n, d):
        xp, zp = plus(x, d), plus(z, d)
        return (
            remote(ra.at[n, xp], ya.at[n, x], p2_ss.at[n, 0, d - 1], p2_rs.at[n, 0, d - 1], xpeer[d - 1]),
            remote(rb.at[n, zp], yb.at[n, z], p2_ss.at[n, 1, d - 1], p2_rs.at[n, 1, d - 1], zpeer[d - 1]),
        )

    def rc(n):
        return remote(
            half.at[lax.rem(n, 2), 1 - c], core_in.at[n], rc_ss.at[n], rc_rs.at[n], core
        )

    def ry(n, d):
        return remote(
            mix.at[n, plus(y, d)], y_in.at[n, d - 1], ry_ss.at[n, d - 1], ry_rs.at[n, d - 1], ypeer[d - 1]
        )

    parity = lax.rem(y, 2)
    pair = place(x, c, z, y + 1 - 2 * parity)
    other = place(x, c, z, plus(y, 3 + 2 * parity))

    def ry_by(n, to, device):
        d = lax.rem(to - y + 4, 4)
        return remote(
            mix.at[n, to], y_in.at[n, d - 1], ry_ss.at[n, d - 1], ry_rs.at[n, d - 1], device
        )

    def ry_pair(n):
        return ry_by(n, y + 1 - 2 * parity, pair)

    def ry_far(n):
        return ry_by(n, plus(y, 3 + 2 * parity), other)

    def swap(f, d):
        i = plus(z, d)
        return remote(sw_out.at[f, i], sw_in.at[f, i], sw_ss.at[f, d], sw_rs.at[f, d], pair)

    def down(i, chunk):
        cols = pl.ds(pl.multiple_of(chunk * CW, CW), CW)
        return jnp.dot(inner[i], wd[:, cols], preferred_element_type=f32)

    order = (1, 2, 3, 0)

    def start_swap(f):
        for d in order:
            i = plus(z, d)
            part = down(i, 2 * f + 1 - parity).astype(bf16)
            sw_out[f, i] = part.reshape(4, SLAB, CW)
            swap(f, d).start()

    load_wd.wait()
    start_swap(0)

    def step(n, carry):
        @pl.when(n < NS - NF)
        def _():
            for i in range(4):
                part = down(i, 2 * NF + n)
                sr[n, i] = part.astype(bf16).reshape(4, SLAB, CW)
            for d in range(1, 4):
                for copy in p1(n, d):
                    copy.start()
            for copy in own(n):
                copy.start()

        @pl.when(n == 0)
        def _():
            for f in range(1, NF):
                start_swap(f)
            find_slots(meta, slots, weights, c, y)
            fill_places(slots, weights, places)

        @pl.when((n >= BACK_AHEAD) & (n < NS + BACK_AHEAD))
        def _():
            i = n - BACK_AHEAD
            for d in range(1, 4):
                for copy in p1(i, d):
                    copy.wait_recv()
            for copy in own(i):
                copy.wait()
            for d in range(1, 4):
                for copy in p2(i, d):
                    copy.start()

        @pl.when((n >= 4) & (n < NS + 4))
        def _():
            m = n - 4
            rc(m).wait_recv()
            mix[m] = (total[lax.rem(m, 2), c] + core_in[m].astype(f32)).astype(bf16)

            @pl.when(m < 2)
            def _():
                ry_far(m).start()

            @pl.when(m == 2)
            def _():
                for i in range(2):
                    ry_pair(i).start()
                    ry(i, 2).start()

            @pl.when(m >= 2)
            def _():
                for d in range(1, 4):
                    ry(m, d).start()

        @pl.when((n >= 3) & (n < NS + 3))
        def _():
            m = n - 3
            loads = [
                pltpu.make_async_copy(ra.at[m, x], rv.at[x, :, :, 0:HW], lsem.at[0]),
                pltpu.make_async_copy(rb.at[m, z], rv.at[:, z, :, HW:CW], lsem.at[1]),
            ]
            for load in loads:
                load.start()
            for d in range(1, 4):
                for copy in p2(m, d):
                    copy.wait_recv()
                zs, xs = plus(z, 4 - d), plus(x, 4 - d)
                more = [
                    pltpu.make_async_copy(ya.at[m, xs], rv.at[xs, :, :, 0:HW], lsem.at[2 * d]),
                    pltpu.make_async_copy(yb.at[m, zs], rv.at[:, zs, :, HW:CW], lsem.at[2 * d + 1]),
                ]
                for load in more:
                    load.start()
                loads += more
            for load in loads:
                load.wait()
            moe = lax.dot_general(
                places[...].reshape(16 * SLAB, 8 * TOK),
                rv[...].reshape(16 * SLAB, CW),
                (((0,), (0,)), ((), ())),
                preferred_element_type=f32,
            )
            total[lax.rem(m, 2)] = moe.reshape(2, 4, TOK, CW)

            @pl.when(m >= 2)
            def _():
                rc(m - 2).wait_send()

            half[lax.rem(m, 2)] = total[lax.rem(m, 2)].astype(bf16)
            rc(m).start()

        @pl.when((n == NS - NF) | (n == NS))
        def _():
            f = (n - (NS - NF)) // 2
            u = NS - NF + f
            for d in order:
                swap(f, d).wait_recv()
                i = plus(z, d)
                part = down(i, 2 * f + parity).reshape(4, SLAB, CW)
                sr[u, i] = (part + sw_in[f, i].astype(f32)).astype(bf16)
                if d > 0:
                    p1_z(u, d).start()
                for e in range(1, 4):
                    p1_part(u, i, e).start()
            for copy in own(u):
                copy.start()

        return carry

    lax.fori_loop(0, NS + 4, step, 0)

    def result(m, carry):
        for d in range(1, 4):
            ry(m, d).wait_recv()
        own_part = mix[m, y].astype(f32)
        one, two, three = [y_in[m, i].astype(f32) for i in range(3)]

        def put(chunk, value):
            cols = pl.ds(pl.multiple_of(chunk * CW, CW), CW)
            out[:, cols] = (resid[:, cols].astype(f32) + value).astype(bf16)

        @pl.when(m < NS - NF)
        def _():
            put(2 * NF + m, own_part + one + two + three)

        @pl.when(m >= NS - NF)
        def _():
            at = 2 * (m - (NS - NF))
            put(at + parity, own_part + two)
            put(at + 1 - parity, one + three)
        return carry

    lax.fori_loop(0, NS, result, 0)

    def finish(n, carry):
        for d in range(1, 4):
            for copy in p1(n, d) + p2(n, d):
                copy.wait_send()
            ry(n, d).wait_send()
        return carry

    lax.fori_loop(0, NS, finish, 0)
    for n in range(NS - 2, NS):
        rc(n).wait_send()
    for f in range(NF):
        for d in range(4):
            swap(f, d).wait_send()


VM = pl.BlockSpec(memory_space=pltpu.VMEM)
ANY = pl.BlockSpec(memory_space=pl.ANY)


def dma(*shape):
    return pltpu.SemaphoreType.DMA(shape)


def params(collective_id):
    return pltpu.CompilerParams(
        collective_id=collective_id, has_side_effects=True, vmem_limit_bytes=62 << 20
    )


def on_device(
    hidden_in, queries, key_rows, value_rows, document_ids, norm_gain,
    w_gate, w_up, w_down, expert_ids, route_weights,
):
    landing = jax.ShapeDtypeStruct((NS, 4, 4, SLAB, HW), bf16)
    swapped = jax.ShapeDtypeStruct((NF, 4, 4, SLAB, HW), bf16)
    resid, meta_all, inner, *_ = pl.pallas_call(
        expert_kernel,
        out_shape=(
            jax.ShapeDtypeStruct((TOK, D), bf16),
            jax.ShapeDtypeStruct((8, 2 * TOPK, TOK), f32),
            jax.ShapeDtypeStruct((4, 4 * SLAB, FF_HALF), bf16),
        ) + (landing,) * 4 + (swapped,) * 2,
        in_specs=[VM] * 8 + [ANY] * 2,
        out_specs=(VM,) * 3 + (ANY,) * 6,
        scratch_shapes=[
            pltpu.VMEM((KV_HEADS, WINDOW, TOK, HEAD_DIM), bf16),
            pltpu.VMEM((KV_HEADS, WINDOW, TOK, HEAD_DIM), bf16),
            pltpu.VMEM((WINDOW, 8, TOK), f32),
            pltpu.VMEM((2 * TOPK, TOK), f32),
            dma(KV_HEADS, 3, 2), dma(KV_HEADS, 3, 2), dma(3), dma(3), dma(7), dma(7),
            pltpu.VMEM((NQ, TOK, CW), bf16),
            pltpu.VMEM((NS, 8, TOK, CW), bf16),
            pltpu.VMEM((16, SLAB, 8 * TOK), bf16),
            pltpu.VMEM((16, 8, TOK), f32),
            pltpu.VMEM((NS, 4, 4, SLAB, HW), bf16),
            pltpu.VMEM((NS, 4, 4, SLAB, HW), bf16),
            pltpu.VMEM((4, 4 * SLAB, FF_HALF), f32),
            pltpu.VMEM((4, 4 * SLAB, FF_HALF), f32),
            pltpu.VMEM((NQ, CW, FF_HALF), bf16),
            pltpu.VMEM((NQ, CW, FF_HALF), bf16),
            pltpu.VMEM((4, 4, SLAB, CW), bf16),
            dma(NS, 3), dma(NS, 3), dma(NS, 4), dma(NS, 4),
            dma(NS, 2, 3), dma(NS, 2, 3), dma(NS, 2, 3), dma(NS, 2, 3),
            dma(NF, 2, 4), dma(NF, 2, 4), dma(NS, 2), dma(2), dma(8),
        ],
        compiler_params=params(0),
    )(
        hidden_in, queries, key_rows, value_rows, document_ids.reshape(1, TOK), expert_ids.T,
        route_weights.T, norm_gain.reshape(1, D),
        w_gate.reshape(NQ, CW, FF_HALF), w_up.reshape(NQ, CW, FF_HALF),
    )

    out, *_ = pl.pallas_call(
        return_kernel,
        out_shape=(jax.ShapeDtypeStruct((TOK, D), bf16),) + (landing,) * 4,
        in_specs=[VM, VM, VM, ANY],
        out_specs=(VM,) + (ANY,) * 4,
        scratch_shapes=[
            pltpu.VMEM((16, SLAB, 8 * TOK), bf16),
            pltpu.VMEM((16, 8, TOK), f32),
            pltpu.VMEM((16, 8, TOK), f32),
            pltpu.VMEM((NS, 4, 4, SLAB, CW), bf16),
            pltpu.VMEM((NF, 4, 4, SLAB, CW), bf16),
            pltpu.VMEM((NF, 4, 4, SLAB, CW), bf16),
            pltpu.VMEM((FF_HALF, D), bf16),
            pltpu.VMEM((4, 4, SLAB, CW), bf16),
            pltpu.VMEM((2, 2, 4, TOK, CW), f32),
            pltpu.VMEM((2, 2, 4, TOK, CW), bf16),
            pltpu.VMEM((NS, 4, TOK, CW), bf16),
            pltpu.VMEM((NS, 4, TOK, CW), bf16),
            pltpu.VMEM((NS, 3, TOK, CW), bf16),
            dma(NS, 2, 3), dma(NS, 2, 3), dma(NS, 2, 3), dma(NS, 2, 3),
            dma(NS), dma(NS), dma(NS, 3), dma(NS, 3),
            dma(NF, 4), dma(NF, 4), dma(NS, 2), pltpu.SemaphoreType.DMA, dma(8),
        ],
        compiler_params=params(1),
    )(inner, meta_all, resid, w_down.reshape(FF_HALF, D))
    return out


def solution(mesh):
    rows = P(("ctx", "exp"), None)
    whole = P(("ctx", "exp"), None, None)
    in_specs = (
        rows, rows, rows, rows, P(("ctx", "exp")), P(), whole, whole, whole, rows, rows,
    )
    return jax.shard_map(
        on_device, mesh=mesh, in_specs=in_specs, out_specs=rows, check_vma=False
    )
```

```python
import jax
import jax.numpy as jnp
from jax import lax
from jax.experimental import pallas as pl
from jax.experimental.pallas import tpu as pltpu
from jax.sharding import PartitionSpec as P

D = 3584
KV_HEADS = 4
HEAD_DIM = 128
TOPK = 8
WINDOW = 4
GROUP = 7
TOK = 128
CAP = 17
FF_HALF = 640
NQ = 7
CW = D // NQ
HW = CW // 2
SLAB = 144
OUT_AHEAD = 1
BACK_AHEAD = 2
NF = 2
NS = NQ - NF

MESH = pl.DeviceIdType.MESH
masked_score = -1e30
bf16 = jnp.bfloat16
f32 = jnp.float32


def coords():
    ctx, ex = lax.axis_index("ctx"), lax.axis_index("exp")
    return ctx // 2, ctx % 2, ex // 4, ex % 4


def place(x, c, z, y):
    return (x * 2 + c, z * 4 + y)


def greet(partners):
    barrier = pltpu.get_barrier_semaphore()
    for partner in partners:
        pl.semaphore_signal(barrier, inc=1, device_id=partner, device_id_type=MESH)
    pl.semaphore_wait(barrier, len(partners))


def remote(src, dst, send_sem, recv_sem, device):
    return pltpu.make_async_remote_copy(
        src_ref=src,
        dst_ref=dst,
        send_sem=send_sem,
        recv_sem=recv_sem,
        device_id=device,
        device_id_type=MESH,
    )


def fetched(n, parity):
    return jnp.where(n < NF, 2 * n + parity, n + NF)


def plus(value, steps):
    return lax.rem(value + steps, 4)


def attend(
    x, c, z, y, rank, hid, q, k, v, doc, ids, route, gain, resid_out, nrm, meta_all,
    kw, vw, docw, meta, halo_ss, halo_rs, doc_ss, doc_rs, meta_ss, meta_rs, by_rank, peers, fills,
):
    mine = c * 4 + y
    row = jnp.broadcast_to(doc[...].astype(f32), (TOK, TOK))
    docw[WINDOW - 1] = row[0:8]
    meta[0:TOPK] = ids[...].astype(f32)
    meta[TOPK:] = route[...]

    def send_doc(d):
        return remote(
            docw.at[WINDOW - 1], docw.at[WINDOW - 1 - d], doc_ss.at[d - 1], doc_rs.at[d - 1], by_rank(d)
        )

    def send_head(g, d):
        cols = pl.ds(g * HEAD_DIM, HEAD_DIM)
        return [
            remote(
                src.at[:, cols], dst.at[g, WINDOW - 1 - d], halo_ss.at[g, d - 1, i], halo_rs.at[g, d - 1, i], by_rank(d)
            )
            for i, (src, dst) in enumerate(((k, kw), (v, vw)))
        ]

    def send_meta(i):
        return remote(meta, meta_all.at[mine], meta_ss.at[i], meta_rs.at[i], peers[i])

    for d in range(1, WINDOW):
        send_doc(d).start()
    def start_head(g):
        for d in range(1, WINDOW):
            for copy in send_head(g, d):
                copy.start()

    start_head(0)
    start_head(1)
    for i in range(7):
        send_meta(i).start()
    meta_all[mine] = meta[...]
    for g in range(KV_HEADS):
        cols = slice(g * HEAD_DIM, (g + 1) * HEAD_DIM)
        kw[g, WINDOW - 1] = k[:, cols]
        vw[g, WINDOW - 1] = v[:, cols]
    for copy in fills:
        copy.wait()
    for d in range(1, WINDOW):
        send_doc(d).wait_recv()

    key_doc = jnp.concatenate([docw[i][0:1, :] for i in range(WINDOW)], 1)
    span = WINDOW * TOK
    column = row.T
    query_doc = jnp.concatenate([column] * WINDOW, 1)
    key_pos = lax.broadcasted_iota(jnp.int32, (TOK, span), 1) + (rank - (WINDOW - 1)) * TOK
    query_pos = lax.broadcasted_iota(jnp.int32, (TOK, span), 0) + rank * TOK
    visible = (query_doc == key_doc) & (key_pos <= query_pos) & (key_pos >= 0)
    square = jnp.zeros((TOK, 1), f32)
    for g in range(KV_HEADS):
        for d in range(1, WINDOW):
            for copy in send_head(g, d):
                copy.wait_recv()
        if g + 2 < KV_HEADS:
            start_head(g + 2)
        keys = kw[g].reshape(span, HEAD_DIM)
        values = vw[g].reshape(span, HEAD_DIM)
        for h in range(GROUP):
            at = (g * GROUP + h) * HEAD_DIM
            here = slice(at, at + HEAD_DIM)
            scores = lax.dot_general(
                q[:, here], keys, (((1,), (1,)), ((), ())), preferred_element_type=f32
            ) * (HEAD_DIM ** -0.5)
            scores = jnp.where(visible, scores, masked_score)
            exps = jnp.exp(scores - jnp.max(scores, 1, keepdims=True))
            probs = (exps / jnp.sum(exps, 1, keepdims=True)).astype(bf16)
            context = jnp.dot(probs, values, preferred_element_type=f32).astype(bf16)
            resid = (hid[:, here].astype(f32) + context.astype(f32)).astype(bf16)
            resid_out[:, here] = resid
            resid_f = resid.astype(f32)
            square += jnp.sum(resid_f * resid_f, 1, keepdims=True)
    inverse = lax.rsqrt(square * (1.0 / D) + 1e-06)
    for n in range(NQ):
        for j in range(CW // HEAD_DIM):
            at = n * CW + j * HEAD_DIM
            value = resid_out[:, at : at + HEAD_DIM].astype(f32) * inverse
            tile = n * (CW // HEAD_DIM) + j
            nrm[n, :, j * HEAD_DIM : (j + 1) * HEAD_DIM] = (value * gain[tile : tile + 1, :]).astype(bf16)
    for i in range(7):
        send_meta(i).wait_recv()

    def finish():
        for d in range(1, WINDOW):
            send_doc(d).wait_send()
        for g in range(KV_HEADS):
            for d in range(1, WINDOW):
                for copy in send_head(g, d):
                    copy.wait_send()
        for i in range(7):
            send_meta(i).wait_send()

    return finish


def find_slots(meta, slots, weights, c, y):
    s = lax.broadcasted_iota(jnp.int32, (16, TOPK, TOK), 0)
    expert = (((s >> 2) * 2 + c) * 8 + (s & 3) * 2 + (y >> 1)).astype(f32)
    earlier = lax.broadcasted_iota(jnp.int32, (TOK, TOK), 0) < lax.broadcasted_iota(
        jnp.int32, (TOK, TOK), 1
    )
    earlier = jnp.where(earlier, 1.0, 0.0).astype(bf16)
    for b in range(8):
        ids = meta[b][0:TOPK, :]
        hit = ids[None] == expert
        member = jnp.sum(jnp.where(hit, 1.0, 0.0), 1)
        before = jnp.dot(member.astype(bf16), earlier, preferred_element_type=f32)
        slots[:, b, :] = jnp.where(member > 0.5, before + float(CAP * b), -1.0)
        if weights is not None:
            weights[:, b, :] = jnp.sum(jnp.where(hit, meta[b][TOPK:, :][None], 0.0), 1)


def fill_places(slots, weights, out):
    def one(s, carry):
        rows = lax.broadcasted_iota(jnp.int32, (SLAB, TOK), 0).astype(f32)
        slot = slots[s]
        weight = None if weights is None else weights[s]
        for b in range(8):
            value = 1.0 if weight is None else weight[b : b + 1, :]
            out[s, :, b * TOK : (b + 1) * TOK] = jnp.where(
                rows == slot[b : b + 1, :], value, 0.0
            ).astype(bf16)
        return carry

    lax.fori_loop(0, 16, one, 0)


def expert_kernel(
    hid_hbm, q_hbm, k, v, doc, ids, route, gain, wg_hbm, wu_hbm,
    resid_out, meta_all, inner_out, ma, mb, xa, xb, pa, pb,
    kw, vw, docw, meta, halo_ss, halo_rs, doc_ss, doc_rs, meta_ss, meta_rs,
    hid, q, resid, inner, isem, rsem, osem, nrm, tok, places, slots, sa, sb, gate, up, wg, wu, xv, xlast,
    ay_ss, ay_rs, ac_ss, ac_rs, p1_ss, p1_rs, p2_ss, p2_rs, sw_ss, sw_rs, loc, wsem, lsem,
):
    x, c, z, y = coords()
    core = place(x, 1 - c, z, y)
    ypeer = [place(x, c, z, plus(y, d)) for d in range(1, 4)]
    xpeer = [place(plus(x, d), c, z, y) for d in range(1, 4)]
    zpeer = [place(x, c, plus(z, d), y) for d in range(1, 4)]
    rank = lax.axis_index("ctx") * 16 + lax.axis_index("exp")

    def by_rank(steps):
        other = lax.rem(rank + steps + 128, 128)
        return (other // 16, lax.rem(other, 16))

    peers = [core] + ypeer + [place(x, 1 - c, z, plus(y, d)) for d in range(1, 4)]
    weights = [
        pltpu.make_async_copy(wg_hbm, wg, wsem.at[0]),
        pltpu.make_async_copy(wu_hbm, wu, wsem.at[1]),
    ]
    fills = [
        pltpu.make_async_copy(q_hbm, q, rsem.at[0]),
        pltpu.make_async_copy(hid_hbm, hid, rsem.at[1]),
    ]
    for copy in fills + weights:
        copy.start()

    greet([by_rank(d) for d in (1, 2, 3, -1, -2, -3)] + peers + xpeer + zpeer)
    finish_attend = attend(
        x, c, z, y, rank, hid, q, k, v, doc, ids, route, gain, resid, nrm, meta_all,
        kw, vw, docw, meta, halo_ss, halo_rs, doc_ss, doc_rs, meta_ss, meta_rs, by_rank, peers, fills,
    )
    save = pltpu.make_async_copy(resid, resid_out, rsem.at[2])
    save.start()
    mine = c * 4 + y
    parity = lax.rem(y, 2)
    pair = place(x, c, z, y + 1 - 2 * parity)

    def ay(n, d):
        src = nrm.at[fetched(n, lax.rem(y + d, 2))]
        return remote(src, tok.at[n, mine], ay_ss.at[n, d - 1], ay_rs.at[n, d - 1], ypeer[d - 1])

    def ac(n, d):
        if d == 0:
            src = nrm.at[fetched(n, parity)]
            at = mine
        else:
            at = c * 4 + plus(y, 4 - d)
            src = tok.at[n, at]
        return remote(src, tok.at[n, at], ac_ss.at[n, d], ac_rs.at[n, d], core)

    def p1_x(n, d):
        xp = plus(x, d)
        return remote(sa.at[n, xp], ma.at[n, :, x], p1_ss.at[n, 0, d - 1], p1_rs.at[n, 0, d - 1], xpeer[d - 1])

    def p1_z(n, d):
        zp = plus(z, d)
        return remote(
            sb.at[n, zp], mb.at[n, :, z], p1_ss.at[n, 1, d - 1], p1_rs.at[n, 1, d - 1], zpeer[d - 1]
        )

    def p1(n, d):
        return p1_x(n, d), p1_z(n, d)

    def own(n):
        return (
            pltpu.make_async_copy(sa.at[n, x], ma.at[n, :, x], loc.at[n, 0]),
            pltpu.make_async_copy(sb.at[n, z], mb.at[n, :, z], loc.at[n, 1]),
        )

    def p2(n, d):
        xp, zp = plus(x, d), plus(z, d)
        return (
            remote(ma.at[n, zp], xa.at[n, z], p2_ss.at[n, 0, d - 1], p2_rs.at[n, 0, d - 1], zpeer[d - 1]),
            remote(mb.at[n, xp], xb.at[n, x], p2_ss.at[n, 1, d - 1], p2_rs.at[n, 1, d - 1], xpeer[d - 1]),
        )

    def p2_last(d):
        n, xp, zp = NS - 1, plus(x, d), plus(z, d)
        return (
            remote(ma.at[n, zp], xlast.at[z, :, :, 0:HW], p2_ss.at[n, 0, d - 1], p2_rs.at[n, 0, d - 1], zpeer[d - 1]),
            remote(mb.at[n, xp], xlast.at[:, x, :, HW:CW], p2_ss.at[n, 1, d - 1], p2_rs.at[n, 1, d - 1], xpeer[d - 1]),
        )

    def own_last():
        n = NS - 1
        return (
            pltpu.make_async_copy(ma.at[n, z], xlast.at[z, :, :, 0:HW], osem.at[0]),
            pltpu.make_async_copy(mb.at[n, x], xlast.at[:, x, :, HW:CW], osem.at[1]),
        )

    def swap(n, d):
        zs, xs = plus(z, 4 - d), plus(x, 4 - d)
        a, b = (ma.at[n, z], mb.at[n, x]) if d == 0 else (xa.at[n, zs], xb.at[n, xs])
        return (
            remote(a, pa.at[n, zs], sw_ss.at[n, 0, d], sw_rs.at[n, 0, d], pair),
            remote(b, pb.at[n, xs], sw_ss.at[n, 1, d], sw_rs.at[n, 1, d], pair),
        )

    def start_gather(n):
        for d in range(1, 4):
            ay(n, d).start()
        ac(n, 0).start()
        tok[n, mine] = nrm[fetched(n, parity)]

    start_gather(0)

    local = pltpu.make_async_copy

    def fetch(i, arriving):
        def arrive(d):
            for copy in p2(i, d):
                copy.wait_recv()

        loads = [
            local(ma.at[i, z], xv.at[z, :, :, 0:HW], lsem.at[0]),
            local(mb.at[i, x], xv.at[:, x, :, HW:CW], lsem.at[1]),
        ]
        for load in loads:
            load.start()
        for d in range(1, 4):
            pl.when(arriving)(lambda: arrive(d))
            zs, xs = plus(z, 4 - d), plus(x, 4 - d)
            more = [
                local(xa.at[i, zs], xv.at[zs, :, :, 0:HW], lsem.at[2 * d]),
                local(xb.at[i, xs], xv.at[:, xs, :, HW:CW], lsem.at[2 * d + 1]),
            ]
            for load in more:
                load.start()
            loads += more
        for load in loads:
            load.wait()

    def forward(n):
        for d in range(1, 4):
            ay(n, d).wait_recv()
            ac(n, d).start()

    find_slots(meta_all, slots, None, c, y)
    fill_places(slots, None, places)
    forward(0)
    start_gather(1)
    gate[...] = jnp.zeros_like(gate)
    up[...] = jnp.zeros_like(up)
    for copy in weights:
        copy.wait()

    def step(n, carry):
        @pl.when(n < NS)
        def _():
            for d in range(4):
                ac(n, d).wait_recv()
            chunk = tok[n].reshape(8 * TOK, CW)
            for d in (1, 2, 3, 0):
                xp = plus(x, d)
                rows = places[pl.ds(xp * 4, 4)].reshape(4 * SLAB, 8 * TOK)
                packed = jnp.dot(rows, chunk, preferred_element_type=f32).astype(bf16)
                packed = packed.reshape(4, SLAB, CW)
                sa[n, xp] = packed[:, :, :HW]
                sb[n, :, xp] = packed[:, :, HW:]
                if d > 0:
                    p1_x(n, d).start()
            for d in range(1, 4):
                p1_z(n, d).start()
            for copy in own(n):
                copy.start()

            @pl.when(n + 1 < NS)
            def _():
                forward(n + 1)

            @pl.when(n + 2 < NS)
            def _():
                start_gather(n + 2)

        @pl.when((n >= OUT_AHEAD) & (n < NS + OUT_AHEAD))
        def _():
            i = n - OUT_AHEAD
            for d in range(1, 4):
                for copy in p1(i, d):
                    copy.wait_recv()
            for copy in own(i):
                copy.wait()

            @pl.when(i < NS - 1)
            def _():
                for d in range(1, 4):
                    for copy in p2(i, d):
                        copy.start()

            @pl.when(i == NS - 1)
            def _():
                for d in range(1, 4):
                    for copy in p2_last(d):
                        copy.start()
                for copy in own_last():
                    copy.start()

            @pl.when(i < NF)
            def _():
                for copy in swap(i, 0):
                    copy.start()

        @pl.when((n > OUT_AHEAD) & (n <= OUT_AHEAD + NF))
        def _():
            i = n - OUT_AHEAD - 1
            for d in range(1, 4):
                for copy in p2(i, d):
                    copy.wait_recv()
                for copy in swap(i, d):
                    copy.start()

        @pl.when(n >= OUT_AHEAD + 2)
        def _():
            m = n - OUT_AHEAD - 2
            swapped = (m == 3) | (m == 5)
            own_step = jnp.where(m < 3, m, m // 2 + 1)
            swap_step = (m - 3) // 2

            @pl.when(jnp.logical_not(swapped))
            def _():
                fetch(own_step, own_step >= NF)

            @pl.when(swapped)
            def _():
                i = swap_step
                for d in range(4):
                    for copy in swap(i, d):
                        copy.wait_recv()
                loads = []
                for d in range(4):
                    loads += [
                        local(pa.at[i, d], xv.at[d, :, :, 0:HW], lsem.at[2 * d]),
                        local(pb.at[i, d], xv.at[:, d, :, HW:CW], lsem.at[2 * d + 1]),
                    ]
                for load in loads:
                    load.start()
                for load in loads:
                    load.wait()

            chunk = fetched(
                jnp.where(swapped, swap_step, own_step), jnp.where(swapped, 1 - parity, parity)
            )
            for i in range(4):
                rows = xv[i].reshape(4 * SLAB, CW)
                gate[i] += jnp.dot(rows, wg[chunk], preferred_element_type=f32)
                up[i] += jnp.dot(rows, wu[chunk], preferred_element_type=f32)

        return carry

    lax.fori_loop(0, NQ + OUT_AHEAD + 1, step, 0)
    for copy in own_last():
        copy.wait()
    for d in range(1, 4):
        for copy in p2_last(d):
            copy.wait_recv()
    results = []
    for i in range(4):
        rows = xlast[i].reshape(4 * SLAB, CW)
        value = gate[i] + jnp.dot(rows, wg[NQ - 1], preferred_element_type=f32)
        other = up[i] + jnp.dot(rows, wu[NQ - 1], preferred_element_type=f32)
        inner[i] = (value / (1.0 + jnp.exp(-value)) * other).astype(bf16)
        results.append(pltpu.make_async_copy(inner.at[i], inner_out.at[i], isem.at[i]))
        results[-1].start()

    def finish(n, carry):
        for d in range(1, 4):
            ay(n, d).wait_send()
            for copy in p1(n, d) + p2(n, d):
                copy.wait_send()
        for d in range(4):
            ac(n, d).wait_send()
        return carry

    lax.fori_loop(0, NS, finish, 0)
    for n in range(NF):
        for d in range(4):
            for copy in swap(n, d):
                copy.wait_send()
    finish_attend()
    save.wait()
    for copy in results:
        copy.wait()


def return_kernel(
    inner_hbm, meta, resid_hbm, wd_hbm,
    out, ra, rb, ya, yb,
    inner, resid, isem, turned, places, slots, weights, sr, sw_out, sw_in, wd, rv, rlast, osem, total, half, core_in, mix, y_in,
    p1_ss, p1_rs, p2_ss, p2_rs, rc_ss, rc_rs, ry_ss, ry_rs, sw_ss, sw_rs, loc, wsem, lsem,
):
    x, c, z, y = coords()
    core = place(x, 1 - c, z, y)
    ypeer = [place(x, c, z, plus(y, d)) for d in range(1, 4)]
    xpeer = [place(plus(x, d), c, z, y) for d in range(1, 4)]
    zpeer = [place(x, c, plus(z, d), y) for d in range(1, 4)]
    load_wd = pltpu.make_async_copy(wd_hbm, wd, wsem)
    load_wd.start()
    load_inner = [
        pltpu.make_async_copy(inner_hbm.at[i], inner.at[i], isem.at[i]) for i in range(4)
    ]
    for load in load_inner:
        load.start()
    load_resid = pltpu.make_async_copy(resid_hbm, resid, isem.at[4])
    load_resid.start()

    def p1_z(n, d):
        zp = plus(z, d)
        return remote(
            sr.at[n, zp, :, :, 0:HW], ra.at[n, :, z], p1_ss.at[n, 0, d - 1], p1_rs.at[n, 0, d - 1], zpeer[d - 1]
        )

    def p1_x(n, d):
        xp = plus(x, d)
        return remote(
            sr.at[n, :, xp, :, HW:CW], rb.at[n, :, x], p1_ss.at[n, 1, d - 1], p1_rs.at[n, 1, d - 1], xpeer[d - 1]
        )

    def p1(n, d):
        return p1_z(n, d), p1_x(n, d)

    def p1_part(n, i, d):
        xp = plus(x, d)
        return remote(
            sr.at[n, i, xp, :, HW:CW], rb.at[n, i, x], p1_ss.at[n, 1, d - 1], p1_rs.at[n, 1, d - 1], xpeer[d - 1]
        )

    def own(n):
        return (
            pltpu.make_async_copy(sr.at[n, z, :, :, 0:HW], ra.at[n, :, z], loc.at[n, 0]),
            pltpu.make_async_copy(sr.at[n, :, x, :, HW:CW], rb.at[n, :, x], loc.at[n, 1]),
        )

    def p2(n, d):
        xp, zp = plus(x, d), plus(z, d)
        return (
            remote(ra.at[n, xp], ya.at[n, x], p2_ss.at[n, 0, d - 1], p2_rs.at[n, 0, d - 1], xpeer[d - 1]),
            remote(rb.at[n, zp], yb.at[n, z], p2_ss.at[n, 1, d - 1], p2_rs.at[n, 1, d - 1], zpeer[d - 1]),
        )

    def p2_last(d):
        n, xp, zp = NS - 1, plus(x, d), plus(z, d)
        return (
            remote(ra.at[n, xp], rlast.at[x, :, :, 0:HW], p2_ss.at[n, 0, d - 1], p2_rs.at[n, 0, d - 1], xpeer[d - 1]),
            remote(rb.at[n, zp], rlast.at[:, z, :, HW:CW], p2_ss.at[n, 1, d - 1], p2_rs.at[n, 1, d - 1], zpeer[d - 1]),
        )

    def own_last():
        n = NS - 1
        return (
            pltpu.make_async_copy(ra.at[n, x], rlast.at[x, :, :, 0:HW], osem.at[0]),
            pltpu.make_async_copy(rb.at[n, z], rlast.at[:, z, :, HW:CW], osem.at[1]),
        )

    def rc(n):
        return remote(
            half.at[lax.rem(n, 2), 1 - c], core_in.at[n], rc_ss.at[n], rc_rs.at[n], core
        )

    def ry(n, d):
        return remote(
            mix.at[n, plus(y, d)], y_in.at[n, d - 1], ry_ss.at[n, d - 1], ry_rs.at[n, d - 1], ypeer[d - 1]
        )

    parity = lax.rem(y, 2)
    pair = place(x, c, z, y + 1 - 2 * parity)
    other = place(x, c, z, plus(y, 3 + 2 * parity))

    def ry_by(n, to, device):
        d = lax.rem(to - y + 4, 4)
        return remote(
            mix.at[n, to], y_in.at[n, d - 1], ry_ss.at[n, d - 1], ry_rs.at[n, d - 1], device
        )

    def ry_pair(n):
        return ry_by(n, y + 1 - 2 * parity, pair)

    def ry_far(n):
        return ry_by(n, plus(y, 3 + 2 * parity), other)

    def swap(f, d):
        i = plus(z, d)
        return remote(sw_out.at[f, i], sw_in.at[f, i], sw_ss.at[f, d], sw_rs.at[f, d], pair)

    def down(i, chunk):
        cols = pl.ds(pl.multiple_of(chunk * CW, CW), CW)
        return jnp.dot(inner[i], wd[:, cols], preferred_element_type=f32)

    order = (1, 2, 3, 0)

    def fill_swap(f, d):
        i = plus(z, d)
        part = down(i, 2 * f + 1 - parity).astype(bf16)
        sw_out[f, i] = part.reshape(4, SLAB, CW)

    load_wd.wait()
    for load in load_inner:
        load.wait()
    def fill_step(n):
        for d in order:
            i = plus(z, d)
            part = down(i, 2 * NF + n)
            sr[n, i] = part.astype(bf16).reshape(4, SLAB, CW)

    for d in order:
        fill_swap(0, d)
    fill_step(0)
    greet([core] + ypeer + xpeer + zpeer)
    for d in order:
        swap(0, d).start()

    def step(n, carry):
        @pl.when(n < NS - NF)
        def _():
            @pl.when(n > 0)
            def _():
                fill_step(n)

            for d in range(1, 4):
                for copy in p1(n, d):
                    copy.start()
            for copy in own(n):
                copy.start()

        @pl.when(n == 0)
        def _():
            for f in range(1, NF):
                for d in order:
                    fill_swap(f, d)
                    swap(f, d).start()
            find_slots(meta, slots, weights, c, y)
            fill_places(slots, weights, places)
            for i in range(2):
                group = places[8 * i : 8 * i + 8].reshape(8 * SLAB, 8 * TOK)
                turned[:, 8 * SLAB * i : 8 * SLAB * (i + 1)] = group.T

        @pl.when((n >= BACK_AHEAD) & (n < NS + BACK_AHEAD))
        def _():
            i = n - BACK_AHEAD
            for d in range(1, 4):
                for copy in p1(i, d):
                    copy.wait_recv()
            for copy in own(i):
                copy.wait()

            @pl.when(i < NS - 1)
            def _():
                for d in range(1, 4):
                    for copy in p2(i, d):
                        copy.start()

            @pl.when(i == NS - 1)
            def _():
                for d in range(1, 4):
                    for copy in p2_last(d):
                        copy.start()
                for copy in own_last():
                    copy.start()

        @pl.when((n >= 4) & (n < NS + 4))
        def _():
            m = n - 4
            rc(m).wait_recv()
            mix[m] = (total[lax.rem(m, 2), c] + core_in[m].astype(f32)).astype(bf16)

            @pl.when(m < 2)
            def _():
                ry_far(m).start()

            @pl.when(m == 2)
            def _():
                for i in range(2):
                    ry_pair(i).start()
                    ry(i, 2).start()

            @pl.when(m >= 2)
            def _():
                for d in range(1, 4):
                    ry(m, d).start()

        @pl.when((n >= 3) & (n < NS + 3))
        def _():
            m = n - 3

            def combine(rows):
                moe = jnp.dot(
                    turned[...], rows[...].reshape(16 * SLAB, CW), preferred_element_type=f32
                )
                total[lax.rem(m, 2)] = moe.reshape(2, 4, TOK, CW)

            @pl.when(m < NS - 1)
            def _():
                loads = [
                    pltpu.make_async_copy(ra.at[m, x], rv.at[x, :, :, 0:HW], lsem.at[0]),
                    pltpu.make_async_copy(rb.at[m, z], rv.at[:, z, :, HW:CW], lsem.at[1]),
                ]
                for load in loads:
                    load.start()
                for d in range(1, 4):
                    for copy in p2(m, d):
                        copy.wait_recv()
                    zs, xs = plus(z, 4 - d), plus(x, 4 - d)
                    more = [
                        pltpu.make_async_copy(ya.at[m, xs], rv.at[xs, :, :, 0:HW], lsem.at[2 * d]),
                        pltpu.make_async_copy(yb.at[m, zs], rv.at[:, zs, :, HW:CW], lsem.at[2 * d + 1]),
                    ]
                    for load in more:
                        load.start()
                    loads += more
                for load in loads:
                    load.wait()
                combine(rv)

            @pl.when(m == NS - 1)
            def _():
                for copy in own_last():
                    copy.wait()
                for d in range(1, 4):
                    for copy in p2_last(d):
                        copy.wait_recv()
                combine(rlast)

            @pl.when(m >= 2)
            def _():
                rc(m - 2).wait_send()

            half[lax.rem(m, 2)] = total[lax.rem(m, 2)].astype(bf16)
            rc(m).start()

        @pl.when((n == NS - NF) | (n == NS))
        def _():
            f = (n - (NS - NF)) // 2
            u = NS - NF + f
            for d in order:
                swap(f, d).wait_recv()
                i = plus(z, d)
                part = down(i, 2 * f + parity).reshape(4, SLAB, CW)
                sr[u, i] = (part + sw_in[f, i].astype(f32)).astype(bf16)
                if d > 0:
                    p1_z(u, d).start()
                for e in range(1, 4):
                    p1_part(u, i, e).start()
            for copy in own(u):
                copy.start()

        return carry

    lax.fori_loop(0, NS + 4, step, 0)
    load_resid.wait()

    def result(m, carry):
        for d in range(1, 4):
            ry(m, d).wait_recv()
        own_part = mix[m, y].astype(f32)
        one, two, three = [y_in[m, i].astype(f32) for i in range(3)]

        def put(chunk, value):
            cols = pl.ds(pl.multiple_of(chunk * CW, CW), CW)
            out[:, cols] = (resid[:, cols].astype(f32) + value).astype(bf16)

        @pl.when(m < NS - NF)
        def _():
            put(2 * NF + m, own_part + one + two + three)

        @pl.when(m >= NS - NF)
        def _():
            at = 2 * (m - (NS - NF))
            put(at + parity, own_part + two)
            put(at + 1 - parity, one + three)
        return carry

    lax.fori_loop(0, NS, result, 0)

    def finish(n, carry):
        for d in range(1, 4):
            for copy in p1(n, d) + p2(n, d):
                copy.wait_send()
            ry(n, d).wait_send()
        return carry

    lax.fori_loop(0, NS, finish, 0)
    for n in range(NS - 2, NS):
        rc(n).wait_send()
    for f in range(NF):
        for d in range(4):
            swap(f, d).wait_send()


VM = pl.BlockSpec(memory_space=pltpu.VMEM)
ANY = pl.BlockSpec(memory_space=pl.ANY)


def dma(*shape):
    return pltpu.SemaphoreType.DMA(shape)


def params(collective_id):
    return pltpu.CompilerParams(
        collective_id=collective_id, has_side_effects=True, vmem_limit_bytes=62 << 20
    )


def on_device(
    hidden_in, queries, key_rows, value_rows, document_ids, norm_gain,
    w_gate, w_up, w_down, expert_ids, route_weights,
):
    landing = jax.ShapeDtypeStruct((NS, 4, 4, SLAB, HW), bf16)
    swapped = jax.ShapeDtypeStruct((NF, 4, 4, SLAB, HW), bf16)
    resid, meta_all, inner, *_ = pl.pallas_call(
        expert_kernel,
        out_shape=(
            jax.ShapeDtypeStruct((TOK, D), bf16),
            jax.ShapeDtypeStruct((8, 2 * TOPK, TOK), f32),
            jax.ShapeDtypeStruct((4, 4 * SLAB, FF_HALF), bf16),
        ) + (landing,) * 4 + (swapped,) * 2,
        in_specs=[ANY] * 2 + [VM] * 6 + [ANY] * 2,
        out_specs=(ANY, VM, ANY) + (ANY,) * 6,
        scratch_shapes=[
            pltpu.VMEM((KV_HEADS, WINDOW, TOK, HEAD_DIM), bf16),
            pltpu.VMEM((KV_HEADS, WINDOW, TOK, HEAD_DIM), bf16),
            pltpu.VMEM((WINDOW, 8, TOK), f32),
            pltpu.VMEM((2 * TOPK, TOK), f32),
            dma(KV_HEADS, 3, 2), dma(KV_HEADS, 3, 2), dma(3), dma(3), dma(7), dma(7),
            pltpu.VMEM((TOK, D), bf16),
            pltpu.VMEM((TOK, D), bf16),
            pltpu.VMEM((TOK, D), bf16),
            pltpu.VMEM((4, 4 * SLAB, FF_HALF), bf16),
            dma(4), dma(3), dma(2),
            pltpu.VMEM((NQ, TOK, CW), bf16),
            pltpu.VMEM((NS, 8, TOK, CW), bf16),
            pltpu.VMEM((16, SLAB, 8 * TOK), bf16),
            pltpu.VMEM((16, 8, TOK), f32),
            pltpu.VMEM((NS, 4, 4, SLAB, HW), bf16),
            pltpu.VMEM((NS, 4, 4, SLAB, HW), bf16),
            pltpu.VMEM((4, 4 * SLAB, FF_HALF), f32),
            pltpu.VMEM((4, 4 * SLAB, FF_HALF), f32),
            pltpu.VMEM((NQ, CW, FF_HALF), bf16),
            pltpu.VMEM((NQ, CW, FF_HALF), bf16),
            pltpu.VMEM((4, 4, SLAB, CW), bf16),
            pltpu.VMEM((4, 4, SLAB, CW), bf16),
            dma(NS, 3), dma(NS, 3), dma(NS, 4), dma(NS, 4),
            dma(NS, 2, 3), dma(NS, 2, 3), dma(NS, 2, 3), dma(NS, 2, 3),
            dma(NF, 2, 4), dma(NF, 2, 4), dma(NS, 2), dma(2), dma(8),
        ],
        compiler_params=params(0),
    )(
        hidden_in, queries, key_rows, value_rows, document_ids.reshape(1, TOK), expert_ids.T,
        route_weights.T, norm_gain.reshape(D // HEAD_DIM, HEAD_DIM),
        w_gate.reshape(NQ, CW, FF_HALF), w_up.reshape(NQ, CW, FF_HALF),
    )

    out, *_ = pl.pallas_call(
        return_kernel,
        out_shape=(jax.ShapeDtypeStruct((TOK, D), bf16),) + (landing,) * 4,
        in_specs=[ANY, VM, ANY, ANY],
        out_specs=(VM,) + (ANY,) * 4,
        scratch_shapes=[
            pltpu.VMEM((4, 4 * SLAB, FF_HALF), bf16),
            pltpu.VMEM((TOK, D), bf16),
            dma(5),
            pltpu.VMEM((8 * TOK, 16 * SLAB), bf16),
            pltpu.VMEM((16, SLAB, 8 * TOK), bf16),
            pltpu.VMEM((16, 8, TOK), f32),
            pltpu.VMEM((16, 8, TOK), f32),
            pltpu.VMEM((NS, 4, 4, SLAB, CW), bf16),
            pltpu.VMEM((NF, 4, 4, SLAB, CW), bf16),
            pltpu.VMEM((NF, 4, 4, SLAB, CW), bf16),
            pltpu.VMEM((FF_HALF, D), bf16),
            pltpu.VMEM((4, 4, SLAB, CW), bf16),
            pltpu.VMEM((4, 4, SLAB, CW), bf16),
            dma(2),
            pltpu.VMEM((2, 2, 4, TOK, CW), f32),
            pltpu.VMEM((2, 2, 4, TOK, CW), bf16),
            pltpu.VMEM((NS, 4, TOK, CW), bf16),
            pltpu.VMEM((NS, 4, TOK, CW), bf16),
            pltpu.VMEM((NS, 3, TOK, CW), bf16),
            dma(NS, 2, 3), dma(NS, 2, 3), dma(NS, 2, 3), dma(NS, 2, 3),
            dma(NS), dma(NS), dma(NS, 3), dma(NS, 3),
            dma(NF, 4), dma(NF, 4), dma(NS, 2), pltpu.SemaphoreType.DMA, dma(8),
        ],
        compiler_params=params(1),
    )(inner, meta_all, resid, w_down.reshape(FF_HALF, D))
    return out


def solution(mesh):
    rows = P(("ctx", "exp"), None)
    whole = P(("ctx", "exp"), None, None)
    in_specs = (
        rows, rows, rows, rows, P(("ctx", "exp")), P(), whole, whole, whole, rows, rows,
    )
    return jax.shard_map(
        on_device, mesh=mesh, in_specs=in_specs, out_specs=rows, check_vma=False
    )
```

```python
import jax
import jax.numpy as jnp
from jax import lax
from jax.experimental import pallas as pl
from jax.experimental.pallas import tpu as pltpu
from jax.sharding import PartitionSpec as P

D = 3584
KV_HEADS = 4
HEAD_DIM = 128
TOPK = 8
WINDOW = 4
GROUP = 7
TOK = 128
CAP = 17
FF_HALF = 640
NQ = 7
CW = D // NQ
HW = CW // 2
SLAB = 144
OUT_AHEAD = 1
BACK_AHEAD = 2
NF = 2
NS = NQ - NF

MESH = pl.DeviceIdType.MESH
masked_score = -1e30
bf16 = jnp.bfloat16
f32 = jnp.float32


def coords():
    ctx, ex = lax.axis_index("ctx"), lax.axis_index("exp")
    return ctx // 2, ctx % 2, ex // 4, ex % 4


def place(x, c, z, y):
    return (x * 2 + c, z * 4 + y)


def greet(partners):
    barrier = pltpu.get_barrier_semaphore()
    for partner in partners:
        pl.semaphore_signal(barrier, inc=1, device_id=partner, device_id_type=MESH)
    pl.semaphore_wait(barrier, len(partners))


def remote(src, dst, send_sem, recv_sem, device):
    return pltpu.make_async_remote_copy(
        src_ref=src,
        dst_ref=dst,
        send_sem=send_sem,
        recv_sem=recv_sem,
        device_id=device,
        device_id_type=MESH,
    )


def fetched(n, parity):
    return jnp.where(n < NF, 2 * n + parity, n + NF)


def plus(value, steps):
    return lax.rem(value + steps, 4)


def attend(
    x, c, z, y, rank, hid, q, k, v, doc, ids, route, gain, resid_out, nrm, meta_all,
    kw, vw, docw, meta, halo_ss, halo_rs, doc_ss, doc_rs, meta_ss, meta_rs, by_rank, peers, fills, when_first,
):
    mine = c * 4 + y
    row = jnp.broadcast_to(doc[...].astype(f32), (TOK, TOK))
    docw[WINDOW - 1] = row[0:8]
    meta[0:TOPK] = ids[...].astype(f32)
    meta[TOPK:] = route[...]

    def send_doc(d):
        return remote(
            docw.at[WINDOW - 1], docw.at[WINDOW - 1 - d], doc_ss.at[d - 1], doc_rs.at[d - 1], by_rank(d)
        )

    def send_head(g, d):
        cols = pl.ds(g * HEAD_DIM, HEAD_DIM)
        return [
            remote(
                src.at[:, cols], dst.at[g, WINDOW - 1 - d], halo_ss.at[g, d - 1, i], halo_rs.at[g, d - 1, i], by_rank(d)
            )
            for i, (src, dst) in enumerate(((k, kw), (v, vw)))
        ]

    def send_meta(i):
        return remote(meta, meta_all.at[mine], meta_ss.at[i], meta_rs.at[i], peers[i])

    for d in range(1, WINDOW):
        send_doc(d).start()
    def start_head(g):
        for d in range(1, WINDOW):
            for copy in send_head(g, d):
                copy.start()

    start_head(0)
    start_head(1)
    for i in range(7):
        send_meta(i).start()
    meta_all[mine] = meta[...]
    for g in range(KV_HEADS):
        cols = slice(g * HEAD_DIM, (g + 1) * HEAD_DIM)
        kw[g, WINDOW - 1] = k[:, cols]
        vw[g, WINDOW - 1] = v[:, cols]
    for copy in fills:
        copy.wait()
    for d in range(1, WINDOW):
        send_doc(d).wait_recv()

    key_doc = jnp.concatenate([docw[i][0:1, :] for i in range(WINDOW)], 1)
    span = WINDOW * TOK
    column = row.T
    query_doc = jnp.concatenate([column] * WINDOW, 1)
    key_pos = lax.broadcasted_iota(jnp.int32, (TOK, span), 1) + (rank - (WINDOW - 1)) * TOK
    query_pos = lax.broadcasted_iota(jnp.int32, (TOK, span), 0) + rank * TOK
    visible = (query_doc == key_doc) & (key_pos <= query_pos) & (key_pos >= 0)
    square = jnp.zeros((TOK, 1), f32)
    for g in range(KV_HEADS):
        for d in range(1, WINDOW):
            for copy in send_head(g, d):
                copy.wait_recv()
        if g + 2 < KV_HEADS:
            start_head(g + 2)
        keys = kw[g].reshape(span, HEAD_DIM)
        values = vw[g].reshape(span, HEAD_DIM)
        for h in range(GROUP):
            at = (g * GROUP + h) * HEAD_DIM
            here = slice(at, at + HEAD_DIM)
            scores = lax.dot_general(
                q[:, here], keys, (((1,), (1,)), ((), ())), preferred_element_type=f32
            ) * (HEAD_DIM ** -0.5)
            scores = jnp.where(visible, scores, masked_score)
            exps = jnp.exp(scores - jnp.max(scores, 1, keepdims=True))
            probs = (exps / jnp.sum(exps, 1, keepdims=True)).astype(bf16)
            context = jnp.dot(probs, values, preferred_element_type=f32).astype(bf16)
            resid = (hid[:, here].astype(f32) + context.astype(f32)).astype(bf16)
            resid_out[:, here] = resid
            resid_f = resid.astype(f32)
            square += jnp.sum(resid_f * resid_f, 1, keepdims=True)
    inverse = lax.rsqrt(square * (1.0 / D) + 1e-06)
    for n in range(NQ):
        for j in range(CW // HEAD_DIM):
            at = n * CW + j * HEAD_DIM
            value = resid_out[:, at : at + HEAD_DIM].astype(f32) * inverse
            tile = n * (CW // HEAD_DIM) + j
            nrm[n, :, j * HEAD_DIM : (j + 1) * HEAD_DIM] = (value * gain[tile : tile + 1, :]).astype(bf16)
        if n == 1:
            when_first()
    for i in range(7):
        send_meta(i).wait_recv()

    def finish():
        for d in range(1, WINDOW):
            send_doc(d).wait_send()
        for g in range(KV_HEADS):
            for d in range(1, WINDOW):
                for copy in send_head(g, d):
                    copy.wait_send()
        for i in range(7):
            send_meta(i).wait_send()

    return finish


def find_slots(meta, slots, weights, c, y):
    s = lax.broadcasted_iota(jnp.int32, (16, TOPK, TOK), 0)
    expert = (((s >> 2) * 2 + c) * 8 + (s & 3) * 2 + (y >> 1)).astype(f32)
    earlier = lax.broadcasted_iota(jnp.int32, (TOK, TOK), 0) < lax.broadcasted_iota(
        jnp.int32, (TOK, TOK), 1
    )
    earlier = jnp.where(earlier, 1.0, 0.0).astype(bf16)
    for b in range(8):
        ids = meta[b][0:TOPK, :]
        hit = ids[None] == expert
        member = jnp.sum(jnp.where(hit, 1.0, 0.0), 1)
        before = jnp.dot(member.astype(bf16), earlier, preferred_element_type=f32)
        slots[:, b, :] = jnp.where(member > 0.5, before + float(CAP * b), -1.0)
        if weights is not None:
            weights[:, b, :] = jnp.sum(jnp.where(hit, meta[b][TOPK:, :][None], 0.0), 1)


def fill_places(slots, weights, out):
    def one(s, carry):
        rows = lax.broadcasted_iota(jnp.int32, (SLAB, TOK), 0).astype(f32)
        slot = slots[s]
        weight = None if weights is None else weights[s]
        for b in range(8):
            value = 1.0 if weight is None else weight[b : b + 1, :]
            out[s, :, b * TOK : (b + 1) * TOK] = jnp.where(
                rows == slot[b : b + 1, :], value, 0.0
            ).astype(bf16)
        return carry

    lax.fori_loop(0, 16, one, 0)


def expert_kernel(
    hid_hbm, q_hbm, k, v, doc, ids, route, gain, wg_hbm, wu_hbm,
    resid_out, meta_all, inner_out, ma, mb, xa, xb, pa, pb,
    kw, vw, docw, meta, halo_ss, halo_rs, doc_ss, doc_rs, meta_ss, meta_rs,
    hid, q, resid, inner, isem, rsem, osem, nrm, tok, places, slots, sa, sb, gate, up, wg, wu, xv, xlast,
    ay_ss, ay_rs, ac_ss, ac_rs, p1_ss, p1_rs, p2_ss, p2_rs, sw_ss, sw_rs, loc, wsem, lsem,
):
    x, c, z, y = coords()
    core = place(x, 1 - c, z, y)
    ypeer = [place(x, c, z, plus(y, d)) for d in range(1, 4)]
    xpeer = [place(plus(x, d), c, z, y) for d in range(1, 4)]
    zpeer = [place(x, c, plus(z, d), y) for d in range(1, 4)]
    rank = lax.axis_index("ctx") * 16 + lax.axis_index("exp")

    def by_rank(steps):
        other = lax.rem(rank + steps + 128, 128)
        return (other // 16, lax.rem(other, 16))

    peers = [core] + ypeer + [place(x, 1 - c, z, plus(y, d)) for d in range(1, 4)]
    weights = [
        pltpu.make_async_copy(wg_hbm, wg, wsem.at[0]),
        pltpu.make_async_copy(wu_hbm, wu, wsem.at[1]),
    ]
    fills = [
        pltpu.make_async_copy(q_hbm, q, rsem.at[0]),
        pltpu.make_async_copy(hid_hbm, hid, rsem.at[1]),
    ]
    for copy in fills + weights:
        copy.start()

    greet([by_rank(d) for d in (1, 2, 3, -1, -2, -3)] + peers + xpeer + zpeer)
    mine = c * 4 + y
    parity = lax.rem(y, 2)
    pair = place(x, c, z, y + 1 - 2 * parity)

    def ay(n, d):
        src = nrm.at[fetched(n, lax.rem(y + d, 2))]
        return remote(src, tok.at[n, mine], ay_ss.at[n, d - 1], ay_rs.at[n, d - 1], ypeer[d - 1])

    def ac(n, d):
        if d == 0:
            src = nrm.at[fetched(n, parity)]
            at = mine
        else:
            at = c * 4 + plus(y, 4 - d)
            src = tok.at[n, at]
        return remote(src, tok.at[n, at], ac_ss.at[n, d], ac_rs.at[n, d], core)

    def p1_x(n, d):
        xp = plus(x, d)
        return remote(sa.at[n, xp], ma.at[n, :, x], p1_ss.at[n, 0, d - 1], p1_rs.at[n, 0, d - 1], xpeer[d - 1])

    def p1_z(n, d):
        zp = plus(z, d)
        return remote(
            sb.at[n, zp], mb.at[n, :, z], p1_ss.at[n, 1, d - 1], p1_rs.at[n, 1, d - 1], zpeer[d - 1]
        )

    def p1(n, d):
        return p1_x(n, d), p1_z(n, d)

    def own(n):
        return (
            pltpu.make_async_copy(sa.at[n, x], ma.at[n, :, x], loc.at[n, 0]),
            pltpu.make_async_copy(sb.at[n, z], mb.at[n, :, z], loc.at[n, 1]),
        )

    def p2(n, d):
        xp, zp = plus(x, d), plus(z, d)
        return (
            remote(ma.at[n, zp], xa.at[n, z], p2_ss.at[n, 0, d - 1], p2_rs.at[n, 0, d - 1], zpeer[d - 1]),
            remote(mb.at[n, xp], xb.at[n, x], p2_ss.at[n, 1, d - 1], p2_rs.at[n, 1, d - 1], xpeer[d - 1]),
        )

    def p2_last(d):
        n, xp, zp = NS - 1, plus(x, d), plus(z, d)
        return (
            remote(ma.at[n, zp], xlast.at[z, :, :, 0:HW], p2_ss.at[n, 0, d - 1], p2_rs.at[n, 0, d - 1], zpeer[d - 1]),
            remote(mb.at[n, xp], xlast.at[:, x, :, HW:CW], p2_ss.at[n, 1, d - 1], p2_rs.at[n, 1, d - 1], xpeer[d - 1]),
        )

    def own_last():
        n = NS - 1
        return (
            pltpu.make_async_copy(ma.at[n, z], xlast.at[z, :, :, 0:HW], osem.at[0]),
            pltpu.make_async_copy(mb.at[n, x], xlast.at[:, x, :, HW:CW], osem.at[1]),
        )

    def swap(n, d):
        zs, xs = plus(z, 4 - d), plus(x, 4 - d)
        a, b = (ma.at[n, z], mb.at[n, x]) if d == 0 else (xa.at[n, zs], xb.at[n, xs])
        return (
            remote(a, pa.at[n, zs], sw_ss.at[n, 0, d], sw_rs.at[n, 0, d], pair),
            remote(b, pb.at[n, xs], sw_ss.at[n, 1, d], sw_rs.at[n, 1, d], pair),
        )

    def start_gather(n):
        for d in (2, 1, 3):
            ay(n, d).start()
        ac(n, 0).start()
        tok[n, mine] = nrm[fetched(n, parity)]

    finish_attend = attend(
        x, c, z, y, rank, hid, q, k, v, doc, ids, route, gain, resid, nrm, meta_all,
        kw, vw, docw, meta, halo_ss, halo_rs, doc_ss, doc_rs, meta_ss, meta_rs, by_rank, peers, fills, lambda: start_gather(0),
    )
    save = pltpu.make_async_copy(resid, resid_out, rsem.at[2])
    save.start()

    local = pltpu.make_async_copy

    def fetch(i, arriving):
        def arrive(d):
            for copy in p2(i, d):
                copy.wait_recv()

        loads = [
            local(ma.at[i, z], xv.at[z, :, :, 0:HW], lsem.at[0]),
            local(mb.at[i, x], xv.at[:, x, :, HW:CW], lsem.at[1]),
        ]
        for load in loads:
            load.start()
        for d in (2, 1, 3):
            pl.when(arriving)(lambda: arrive(d))
            zs, xs = plus(z, 4 - d), plus(x, 4 - d)
            more = [
                local(xa.at[i, zs], xv.at[zs, :, :, 0:HW], lsem.at[2 * d]),
                local(xb.at[i, xs], xv.at[:, xs, :, HW:CW], lsem.at[2 * d + 1]),
            ]
            for load in more:
                load.start()
            loads += more
        for load in loads:
            load.wait()

    def forward(n):
        for d in (2, 1, 3):
            ay(n, d).wait_recv()
            ac(n, d).start()

    find_slots(meta_all, slots, None, c, y)
    fill_places(slots, None, places)
    forward(0)
    start_gather(1)
    gate[...] = jnp.zeros_like(gate)
    up[...] = jnp.zeros_like(up)
    for copy in weights:
        copy.wait()

    def step(n, carry):
        @pl.when(n < NS)
        def _():
            for d in range(4):
                ac(n, d).wait_recv()
            chunk = tok[n].reshape(8 * TOK, CW)
            for d in (2, 1, 3, 0):
                xp = plus(x, d)
                rows = places[pl.ds(xp * 4, 4)].reshape(4 * SLAB, 8 * TOK)
                packed = jnp.dot(rows, chunk, preferred_element_type=f32).astype(bf16)
                packed = packed.reshape(4, SLAB, CW)
                sa[n, xp] = packed[:, :, :HW]
                sb[n, :, xp] = packed[:, :, HW:]
                if d > 0:
                    p1_x(n, d).start()
            for d in (2, 1, 3):
                p1_z(n, d).start()
            for copy in own(n):
                copy.start()

            @pl.when(n + 1 < NS)
            def _():
                forward(n + 1)

            @pl.when(n + 2 < NS)
            def _():
                start_gather(n + 2)

        @pl.when((n >= OUT_AHEAD) & (n < NS + OUT_AHEAD))
        def _():
            i = n - OUT_AHEAD
            for d in (2, 1, 3):
                for copy in p1(i, d):
                    copy.wait_recv()
            for copy in own(i):
                copy.wait()

            @pl.when(i < NS - 1)
            def _():
                for d in (2, 1, 3):
                    for copy in p2(i, d):
                        copy.start()

            @pl.when(i == NS - 1)
            def _():
                for d in (2, 1, 3):
                    for copy in p2_last(d):
                        copy.start()
                for copy in own_last():
                    copy.start()

            @pl.when(i < NF)
            def _():
                for copy in swap(i, 0):
                    copy.start()

        @pl.when((n > OUT_AHEAD) & (n <= OUT_AHEAD + NF))
        def _():
            i = n - OUT_AHEAD - 1
            for d in (2, 1, 3):
                for copy in p2(i, d):
                    copy.wait_recv()
                for copy in swap(i, d):
                    copy.start()

        @pl.when(n >= OUT_AHEAD + 2)
        def _():
            m = n - OUT_AHEAD - 2
            swapped = (m == 3) | (m == 5)
            own_step = jnp.where(m < 3, m, m // 2 + 1)
            swap_step = (m - 3) // 2

            @pl.when(jnp.logical_not(swapped))
            def _():
                fetch(own_step, own_step >= NF)

            @pl.when(swapped)
            def _():
                i = swap_step
                for d in range(4):
                    for copy in swap(i, d):
                        copy.wait_recv()
                loads = []
                for d in range(4):
                    loads += [
                        local(pa.at[i, d], xv.at[d, :, :, 0:HW], lsem.at[2 * d]),
                        local(pb.at[i, d], xv.at[:, d, :, HW:CW], lsem.at[2 * d + 1]),
                    ]
                for load in loads:
                    load.start()
                for load in loads:
                    load.wait()

            chunk = fetched(
                jnp.where(swapped, swap_step, own_step), jnp.where(swapped, 1 - parity, parity)
            )
            for i in range(4):
                rows = xv[i].reshape(4 * SLAB, CW)
                gate[i] += jnp.dot(rows, wg[chunk], preferred_element_type=f32)
                up[i] += jnp.dot(rows, wu[chunk], preferred_element_type=f32)

        return carry

    lax.fori_loop(0, NQ + OUT_AHEAD + 1, step, 0)
    for copy in own_last():
        copy.wait()
    for d in (2, 1, 3):
        for copy in p2_last(d):
            copy.wait_recv()
    results = []
    for i in range(4):
        rows = xlast[i].reshape(4 * SLAB, CW)
        value = gate[i] + jnp.dot(rows, wg[NQ - 1], preferred_element_type=f32)
        other = up[i] + jnp.dot(rows, wu[NQ - 1], preferred_element_type=f32)
        inner[i] = (value / (1.0 + jnp.exp(-value)) * other).astype(bf16)
        results.append(pltpu.make_async_copy(inner.at[i], inner_out.at[i], isem.at[i]))
        results[-1].start()

    def finish(n, carry):
        for d in (2, 1, 3):
            ay(n, d).wait_send()
            for copy in p1(n, d) + p2(n, d):
                copy.wait_send()
        for d in range(4):
            ac(n, d).wait_send()
        return carry

    lax.fori_loop(0, NS, finish, 0)
    for n in range(NF):
        for d in range(4):
            for copy in swap(n, d):
                copy.wait_send()
    finish_attend()
    save.wait()
    for copy in results:
        copy.wait()


def return_kernel(
    inner_hbm, meta, resid_hbm, wd_hbm,
    out, ra, rb, ya, yb,
    inner, resid, isem, turned, places, slots, weights, sa, sb, sw_out, sw_in, wd, rv, rlast, osem, total, half, core_in, mix, y_in,
    p1_ss, p1_rs, p2_ss, p2_rs, rc_ss, rc_rs, ry_ss, ry_rs, sw_ss, sw_rs, loc, wsem, lsem,
):
    x, c, z, y = coords()
    core = place(x, 1 - c, z, y)
    ypeer = [place(x, c, z, plus(y, d)) for d in range(1, 4)]
    xpeer = [place(plus(x, d), c, z, y) for d in range(1, 4)]
    zpeer = [place(x, c, plus(z, d), y) for d in range(1, 4)]
    load_wd = pltpu.make_async_copy(wd_hbm, wd, wsem)
    load_wd.start()
    load_inner = [
        pltpu.make_async_copy(inner_hbm.at[i], inner.at[i], isem.at[i]) for i in range(4)
    ]
    for load in load_inner:
        load.start()
    load_resid = pltpu.make_async_copy(resid_hbm, resid, isem.at[4])
    load_resid.start()

    def p1_z(n, d):
        zp = plus(z, d)
        return remote(
            sa.at[n, zp], ra.at[n, :, z], p1_ss.at[n, 0, d - 1], p1_rs.at[n, 0, d - 1], zpeer[d - 1]
        )

    def p1_x(n, d):
        xp = plus(x, d)
        return remote(
            sb.at[n, xp], rb.at[n, :, x], p1_ss.at[n, 1, d - 1], p1_rs.at[n, 1, d - 1], xpeer[d - 1]
        )

    def p1(n, d):
        return p1_z(n, d), p1_x(n, d)

    def p1_part(n, i, d):
        xp = plus(x, d)
        return remote(
            sb.at[n, xp, i], rb.at[n, i, x], p1_ss.at[n, 1, d - 1], p1_rs.at[n, 1, d - 1], xpeer[d - 1]
        )

    def own(n):
        return (
            pltpu.make_async_copy(sa.at[n, z], ra.at[n, :, z], loc.at[n, 0]),
            pltpu.make_async_copy(sb.at[n, x], rb.at[n, :, x], loc.at[n, 1]),
        )

    def p2(n, d):
        xp, zp = plus(x, d), plus(z, d)
        return (
            remote(ra.at[n, xp], ya.at[n, x], p2_ss.at[n, 0, d - 1], p2_rs.at[n, 0, d - 1], xpeer[d - 1]),
            remote(rb.at[n, zp], yb.at[n, z], p2_ss.at[n, 1, d - 1], p2_rs.at[n, 1, d - 1], zpeer[d - 1]),
        )

    def p2_last(d):
        n, xp, zp = NS - 1, plus(x, d), plus(z, d)
        return (
            remote(ra.at[n, xp], rlast.at[x, :, :, 0:HW], p2_ss.at[n, 0, d - 1], p2_rs.at[n, 0, d - 1], xpeer[d - 1]),
            remote(rb.at[n, zp], rlast.at[:, z, :, HW:CW], p2_ss.at[n, 1, d - 1], p2_rs.at[n, 1, d - 1], zpeer[d - 1]),
        )

    def own_last():
        n = NS - 1
        return (
            pltpu.make_async_copy(ra.at[n, x], rlast.at[x, :, :, 0:HW], osem.at[0]),
            pltpu.make_async_copy(rb.at[n, z], rlast.at[:, z, :, HW:CW], osem.at[1]),
        )

    def rc(n):
        return remote(
            half.at[lax.rem(n, 2), 1 - c], core_in.at[n], rc_ss.at[n], rc_rs.at[n], core
        )

    def ry(n, d):
        return remote(
            mix.at[n, plus(y, d)], y_in.at[n, d - 1], ry_ss.at[n, d - 1], ry_rs.at[n, d - 1], ypeer[d - 1]
        )

    parity = lax.rem(y, 2)
    pair = place(x, c, z, y + 1 - 2 * parity)
    other = place(x, c, z, plus(y, 3 + 2 * parity))

    def ry_by(n, to, device):
        d = lax.rem(to - y + 4, 4)
        return remote(
            mix.at[n, to], y_in.at[n, d - 1], ry_ss.at[n, d - 1], ry_rs.at[n, d - 1], device
        )

    def ry_pair(n):
        return ry_by(n, y + 1 - 2 * parity, pair)

    def ry_far(n):
        return ry_by(n, plus(y, 3 + 2 * parity), other)

    def swap(f, d):
        i = plus(z, d)
        return remote(sw_out.at[f, i], sw_in.at[f, i], sw_ss.at[f, d], sw_rs.at[f, d], pair)

    def down(i, chunk):
        cols = pl.ds(pl.multiple_of(chunk * CW, CW), CW)
        return jnp.dot(inner[i], wd[:, cols], preferred_element_type=f32)

    order = (2, 1, 3, 0)

    def fill_swap(f, d):
        i = plus(z, d)
        part = down(i, 2 * f + 1 - parity).astype(bf16)
        sw_out[f, i] = part.reshape(4, SLAB, CW)

    load_wd.wait()
    for load in load_inner:
        load.wait()
    def fill_step(n):
        for d in order:
            i = plus(z, d)
            part = down(i, 2 * NF + n).astype(bf16).reshape(4, SLAB, CW)
            sa[n, i] = part[:, :, :HW]
            sb[n, :, i] = part[:, :, HW:]

    for d in order:
        fill_swap(0, d)
    fill_step(0)
    greet([core] + ypeer + xpeer + zpeer)
    for d in order:
        swap(0, d).start()

    def step(n, carry):
        @pl.when(n < NS - NF)
        def _():
            @pl.when(n > 0)
            def _():
                fill_step(n)

            for d in (2, 1, 3):
                for copy in p1(n, d):
                    copy.start()
            for copy in own(n):
                copy.start()

        @pl.when(n == 0)
        def _():
            for f in range(1, NF):
                for d in order:
                    fill_swap(f, d)
                    swap(f, d).start()
            find_slots(meta, slots, weights, c, y)
            fill_places(slots, weights, places)
            for i in range(2):
                group = places[8 * i : 8 * i + 8].reshape(8 * SLAB, 8 * TOK)
                turned[:, 8 * SLAB * i : 8 * SLAB * (i + 1)] = group.T

        @pl.when((n >= BACK_AHEAD) & (n < NS + BACK_AHEAD))
        def _():
            i = n - BACK_AHEAD
            for d in (2, 1, 3):
                for copy in p1(i, d):
                    copy.wait_recv()
            for copy in own(i):
                copy.wait()

            @pl.when(i < NS - 1)
            def _():
                for d in (2, 1, 3):
                    for copy in p2(i, d):
                        copy.start()

            @pl.when(i == NS - 1)
            def _():
                for d in (2, 1, 3):
                    for copy in p2_last(d):
                        copy.start()
                for copy in own_last():
                    copy.start()

        @pl.when((n == NS - NF) | (n == NS))
        def _():
            f = (n - (NS - NF)) // 2
            u = NS - NF + f
            for d in order:
                swap(f, d).wait_recv()
                i = plus(z, d)
                part = down(i, 2 * f + parity).reshape(4, SLAB, CW)
                part = (part + sw_in[f, i].astype(f32)).astype(bf16)
                sa[u, i] = part[:, :, :HW]
                sb[u, :, i] = part[:, :, HW:]
                if d > 0:
                    p1_z(u, d).start()
                for e in range(1, 4):
                    p1_part(u, i, e).start()
            for copy in own(u):
                copy.start()

        @pl.when((n >= 4) & (n < NS + 4))
        def _():
            m = n - 4
            rc(m).wait_recv()
            mix[m] = (total[lax.rem(m, 2), c] + core_in[m].astype(f32)).astype(bf16)

            @pl.when(m < 2)
            def _():
                ry_far(m).start()

            @pl.when(m == 2)
            def _():
                for i in range(2):
                    ry_pair(i).start()
                    ry(i, 2).start()

            @pl.when(m >= 2)
            def _():
                for d in (2, 1, 3):
                    ry(m, d).start()

        @pl.when((n >= 3) & (n < NS + 3))
        def _():
            m = n - 3

            def combine(rows):
                moe = jnp.dot(
                    turned[...], rows[...].reshape(16 * SLAB, CW), preferred_element_type=f32
                )
                total[lax.rem(m, 2)] = moe.reshape(2, 4, TOK, CW)

            @pl.when(m < NS - 1)
            def _():
                loads = [
                    pltpu.make_async_copy(ra.at[m, x], rv.at[x, :, :, 0:HW], lsem.at[0]),
                    pltpu.make_async_copy(rb.at[m, z], rv.at[:, z, :, HW:CW], lsem.at[1]),
                ]
                for load in loads:
                    load.start()
                for d in (2, 1, 3):
                    for copy in p2(m, d):
                        copy.wait_recv()
                    zs, xs = plus(z, 4 - d), plus(x, 4 - d)
                    more = [
                        pltpu.make_async_copy(ya.at[m, xs], rv.at[xs, :, :, 0:HW], lsem.at[2 * d]),
                        pltpu.make_async_copy(yb.at[m, zs], rv.at[:, zs, :, HW:CW], lsem.at[2 * d + 1]),
                    ]
                    for load in more:
                        load.start()
                    loads += more
                for load in loads:
                    load.wait()
                combine(rv)

            @pl.when(m == NS - 1)
            def _():
                for copy in own_last():
                    copy.wait()
                for d in (2, 1, 3):
                    for copy in p2_last(d):
                        copy.wait_recv()
                combine(rlast)

            @pl.when(m >= 2)
            def _():
                rc(m - 2).wait_send()

            half[lax.rem(m, 2)] = total[lax.rem(m, 2)].astype(bf16)
            rc(m).start()

        return carry

    lax.fori_loop(0, NS + 4, step, 0)
    load_resid.wait()

    def result(m, carry):
        for d in (2, 1, 3):
            ry(m, d).wait_recv()
        own_part = mix[m, y].astype(f32)
        one, two, three = [y_in[m, i].astype(f32) for i in range(3)]

        def put(chunk, value):
            cols = pl.ds(pl.multiple_of(chunk * CW, CW), CW)
            out[:, cols] = (resid[:, cols].astype(f32) + value).astype(bf16)

        @pl.when(m < NS - NF)
        def _():
            put(2 * NF + m, own_part + one + two + three)

        @pl.when(m >= NS - NF)
        def _():
            at = 2 * (m - (NS - NF))
            put(at + parity, own_part + two)
            put(at + 1 - parity, one + three)
        return carry

    lax.fori_loop(0, NS, result, 0)

    def finish(n, carry):
        for d in (2, 1, 3):
            for copy in p1(n, d) + p2(n, d):
                copy.wait_send()
            ry(n, d).wait_send()
        return carry

    lax.fori_loop(0, NS, finish, 0)
    for n in range(NS - 2, NS):
        rc(n).wait_send()
    for f in range(NF):
        for d in range(4):
            swap(f, d).wait_send()


VM = pl.BlockSpec(memory_space=pltpu.VMEM)
ANY = pl.BlockSpec(memory_space=pl.ANY)


def dma(*shape):
    return pltpu.SemaphoreType.DMA(shape)


def params(collective_id):
    return pltpu.CompilerParams(
        collective_id=collective_id, has_side_effects=True, vmem_limit_bytes=62 << 20
    )


def on_device(
    hidden_in, queries, key_rows, value_rows, document_ids, norm_gain,
    w_gate, w_up, w_down, expert_ids, route_weights,
):
    landing = jax.ShapeDtypeStruct((NS, 4, 4, SLAB, HW), bf16)
    swapped = jax.ShapeDtypeStruct((NF, 4, 4, SLAB, HW), bf16)
    resid, meta_all, inner, *_ = pl.pallas_call(
        expert_kernel,
        out_shape=(
            jax.ShapeDtypeStruct((TOK, D), bf16),
            jax.ShapeDtypeStruct((8, 2 * TOPK, TOK), f32),
            jax.ShapeDtypeStruct((4, 4 * SLAB, FF_HALF), bf16),
        ) + (landing,) * 4 + (swapped,) * 2,
        in_specs=[ANY] * 2 + [VM] * 6 + [ANY] * 2,
        out_specs=(ANY, VM, ANY) + (ANY,) * 6,
        scratch_shapes=[
            pltpu.VMEM((KV_HEADS, WINDOW, TOK, HEAD_DIM), bf16),
            pltpu.VMEM((KV_HEADS, WINDOW, TOK, HEAD_DIM), bf16),
            pltpu.VMEM((WINDOW, 8, TOK), f32),
            pltpu.VMEM((2 * TOPK, TOK), f32),
            dma(KV_HEADS, 3, 2), dma(KV_HEADS, 3, 2), dma(3), dma(3), dma(7), dma(7),
            pltpu.VMEM((TOK, D), bf16),
            pltpu.VMEM((TOK, D), bf16),
            pltpu.VMEM((TOK, D), bf16),
            pltpu.VMEM((4, 4 * SLAB, FF_HALF), bf16),
            dma(4), dma(3), dma(2),
            pltpu.VMEM((NQ, TOK, CW), bf16),
            pltpu.VMEM((NS, 8, TOK, CW), bf16),
            pltpu.VMEM((16, SLAB, 8 * TOK), bf16),
            pltpu.VMEM((16, 8, TOK), f32),
            pltpu.VMEM((NS, 4, 4, SLAB, HW), bf16),
            pltpu.VMEM((NS, 4, 4, SLAB, HW), bf16),
            pltpu.VMEM((4, 4 * SLAB, FF_HALF), f32),
            pltpu.VMEM((4, 4 * SLAB, FF_HALF), f32),
            pltpu.VMEM((NQ, CW, FF_HALF), bf16),
            pltpu.VMEM((NQ, CW, FF_HALF), bf16),
            pltpu.VMEM((4, 4, SLAB, CW), bf16),
            pltpu.VMEM((4, 4, SLAB, CW), bf16),
            dma(NS, 3), dma(NS, 3), dma(NS, 4), dma(NS, 4),
            dma(NS, 2, 3), dma(NS, 2, 3), dma(NS, 2, 3), dma(NS, 2, 3),
            dma(NF, 2, 4), dma(NF, 2, 4), dma(NS, 2), dma(2), dma(8),
        ],
        compiler_params=params(0),
    )(
        hidden_in, queries, key_rows, value_rows, document_ids.reshape(1, TOK), expert_ids.T,
        route_weights.T, norm_gain.reshape(D // HEAD_DIM, HEAD_DIM),
        w_gate.reshape(NQ, CW, FF_HALF), w_up.reshape(NQ, CW, FF_HALF),
    )

    out, *_ = pl.pallas_call(
        return_kernel,
        out_shape=(jax.ShapeDtypeStruct((TOK, D), bf16),) + (landing,) * 4,
        in_specs=[ANY, VM, ANY, ANY],
        out_specs=(VM,) + (ANY,) * 4,
        scratch_shapes=[
            pltpu.VMEM((4, 4 * SLAB, FF_HALF), bf16),
            pltpu.VMEM((TOK, D), bf16),
            dma(5),
            pltpu.VMEM((8 * TOK, 16 * SLAB), bf16),
            pltpu.VMEM((16, SLAB, 8 * TOK), bf16),
            pltpu.VMEM((16, 8, TOK), f32),
            pltpu.VMEM((16, 8, TOK), f32),
            pltpu.VMEM((NS, 4, 4, SLAB, HW), bf16),
            pltpu.VMEM((NS, 4, 4, SLAB, HW), bf16),
            pltpu.VMEM((NF, 4, 4, SLAB, CW), bf16),
            pltpu.VMEM((NF, 4, 4, SLAB, CW), bf16),
            pltpu.VMEM((FF_HALF, D), bf16),
            pltpu.VMEM((4, 4, SLAB, CW), bf16),
            pltpu.VMEM((4, 4, SLAB, CW), bf16),
            dma(2),
            pltpu.VMEM((2, 2, 4, TOK, CW), f32),
            pltpu.VMEM((2, 2, 4, TOK, CW), bf16),
            pltpu.VMEM((NS, 4, TOK, CW), bf16),
            pltpu.VMEM((NS, 4, TOK, CW), bf16),
            pltpu.VMEM((NS, 3, TOK, CW), bf16),
            dma(NS, 2, 3), dma(NS, 2, 3), dma(NS, 2, 3), dma(NS, 2, 3),
            dma(NS), dma(NS), dma(NS, 3), dma(NS, 3),
            dma(NF, 4), dma(NF, 4), dma(NS, 2), pltpu.SemaphoreType.DMA, dma(8),
        ],
        compiler_params=params(1),
    )(inner, meta_all, resid, w_down.reshape(FF_HALF, D))
    return out


def solution(mesh):
    rows = P(("ctx", "exp"), None)
    whole = P(("ctx", "exp"), None, None)
    in_specs = (
        rows, rows, rows, rows, P(("ctx", "exp")), P(), whole, whole, whole, rows, rows,
    )
    return jax.shard_map(
        on_device, mesh=mesh, in_specs=in_specs, out_specs=rows, check_vma=False
    )
```
